32 devices in a mesh: expert: 8 (over z, y), tensor: 4 (over x, core).
Axes of the slice: x: 2, y: 2, z: 4, core: 2. Of those that a mesh axis runs over, the one named last changes fastest.
Arguments:
- tokens: bfloat16 [8192, 768], P('expert'), may hold values from -6 to 6
- cotangent: bfloat16 [8192, 768], P('expert'), may hold values from -6 to 6
- gain_attn: bfloat16 [768], replicated, may hold values from 0.099609375 to 1.8984375
- gain_ffn: bfloat16 [768], replicated, may hold values from 0.099609375 to 1.8984375
- w_qkv: bfloat16 [3, 768, 768], P(None, None, 'tensor'), may hold values from -0.21875 to 0.21875
- w_out: bfloat16 [768, 768], P('tensor'), may hold values from -0.875 to 0.875
- bias_table: bfloat16 [32, 12], P(None, 'tensor'), may hold values from -4 to 4
- router: bfloat16 [768, 8], replicated, may hold values from -0.15625 to 0.15625
- w_in: bfloat16 [8, 768, 3072], P('expert', None, 'tensor'), may hold values from -0.21875 to 0.21875
- w_down: bfloat16 [8, 3072, 768], P('expert', 'tensor'), may hold values from -0.109375 to 0.109375
- routes: int32 [8192, 2], P('expert'), may hold values from 0 to 7, all different within a row; in each aligned block of 1024 rows (0 to 1023, 1024 to 2047, ...) at most 512 rows name the same one
- sequence_ids: int32 [8192], P('expert'), may hold values from 0 to 1023, as said below
- rel_buckets: int32 [1024], replicated, may hold values from 0 to 31, as said below
Outputs:
- output_rows: bfloat16 [8192, 768], P('expert')
- d_tokens: bfloat16 [8192, 768], P('expert')
- d_gain_attn: float32 [768], replicated
- d_gain_ffn: float32 [768], replicated
- d_qkv: float32 [3, 768, 768], P(None, None, 'tensor')
- d_out: float32 [768, 768], P('tensor')
- d_bias: float32 [32, 12], P(None, 'tensor')
- d_router: float32 [768, 8], replicated
- d_w_in: float32 [8, 768, 3072], P('expert', None, 'tensor')
- d_w_down: float32 [8, 3072, 768], P('expert', 'tensor')
The draws below stay inside these ranges and needn't reach their ends.
Inputs may be any that keep to these rules, and one draw needn't show every extreme that they name: `routes`: each token names two different experts. Among the 1024 tokens of one device no expert is named more than 512 times, and in every draw some expert is named exactly 512 times by one device's tokens. `sequence_ids`: on each device the numbers of its 1024 tokens start at 0 and never fall, and may skip values; equal numbers on one device form one sequence. On some device all 1024 tokens form one sequence; on some device the last token alone has the number 1024 - 1. `rel_buckets`: entry d is the bucket of a key d positions before its query; it is 0 at d = 0, never falls, and is 31 at d = 1023.
All inputs are finite; a program needn't handle non-finite values.
Results may differ from the reference program's by a relative error of at most 0.018.
Values may be sent and summed in bfloat16 or wider, within the bound.
No kernel may reach another device: no remote copies, remote signals or barrier semaphores. Data moves between devices by JAX's collectives and lax.ppermute only.
A program may use at most 192 MiB of HBM per device.

```python
import math
import jax
import jax.numpy as jnp
import numpy as np
from jax import lax

D = 768
HEADS = 12
HK = 64
FF = 3072
NB = 32
TOK_DEV = 1024
EXPERTS = 8
HD = 768
CAP = 512
TOKENS = 8192
N_EXPERT = 8
N_TENSOR = 4


def draw_sequence_ids(key, part):
    key = jax.random.fold_in(key, 11)
    first_key, second_key, third_key = jax.random.split(key, 3)
    blocks = TOKENS // TOK_DEV
    spacing = jax.random.randint(first_key, (blocks, 1), 8, TOK_DEV // 2 + 1)
    ticket = jax.random.randint(second_key, (blocks, TOK_DEV), 0, 1 << 20)
    breaks = (ticket % spacing == 0).astype(jnp.int32)
    whole_device = jax.random.randint(third_key, (), 0, blocks)
    other_device = (whole_device + 1) % blocks
    block_rows = jnp.arange(blocks)[:, None]
    places = jnp.arange(TOK_DEV)[None, :]
    last_place = (block_rows == other_device) & (places == TOK_DEV - 1)
    breaks = jnp.where(last_place, 1, breaks)
    breaks = jnp.where(block_rows == whole_device, 0, breaks)
    breaks = jnp.where(places == 0, 0, breaks)
    numbers = jnp.cumsum(breaks, axis=1)
    numbers = jnp.where(last_place, TOK_DEV - 1, numbers)
    return numbers.astype(jnp.int32).reshape(-1)


def draw_rel_buckets(key, part):
    key = jax.random.fold_in(key, 23)
    positions = jnp.arange(TOK_DEV)
    exact_count = NB // 2
    spacing = max((TOK_DEV - exact_count) // exact_count, 1)
    ticket = jax.random.randint(key, (TOK_DEV,), 0, spacing)
    steps_up = jnp.where(positions < exact_count, 1, (ticket == 0).astype(jnp.int32))
    steps_up = jnp.where(positions == 0, 0, steps_up)
    bucket_rows = jnp.minimum(jnp.cumsum(steps_up), NB - 1)
    bucket_rows = jnp.where(positions == TOK_DEV - 1, NB - 1, bucket_rows)
    return bucket_rows.astype(jnp.int32)


def levels(key, shape, pieces, low, high):
    loudness, own = 1.0, jax.random.fold_in(key, 6)
    for axis_at, blocks in pieces:
        steps = jnp.exp(jax.random.uniform(jax.random.fold_in(own, axis_at), (blocks,), jnp.float32, low / len(pieces), high / len(pieces)))
        loudness = loudness * jnp.repeat(steps, shape[axis_at] // blocks).reshape([-1 if axis == axis_at else 1 for axis in range(len(shape))])
    return loudness


def shared_out(key, own, number, rows, number_of, top, limit, lean):
    sequence = jax.random.permutation(key, number_of)
    heavy_load, common = shares(number_of, rows * top, limit, lean, True), shares(number_of, rows * top, limit, lean, False)
    places = jnp.arange(number_of)

    def named(tallies, turn):
        used = int((tallies > 0).sum())
        fixed = max(1, used // 4)
        moved = fixed + (places - fixed + turn * (used - fixed)) % max(1, number_of - fixed)
        return jnp.zeros((number_of,), jnp.int32).at[sequence[jnp.where(places < fixed, places, moved)]].set(jnp.asarray(tallies, jnp.int32))

    tallies = jnp.where(number % 4 == 0, named(heavy_load, number // 4), named(common, number - number // 4 - 1))
    mixed = jax.random.permutation(jax.random.fold_in(own, 3), number_of)
    source_of, taker = mixed[0:number_of // 2 * 2:2], mixed[1:number_of // 2 * 2:2]
    slack = jnp.minimum(tallies[source_of] - 1, limit - tallies[taker]) // 2
    slack = jnp.where((source_of == sequence[0]) | (taker == sequence[0]) | (tallies[taker] == 0), 0, jnp.maximum(slack, 0))
    moved = jax.random.randint(jax.random.fold_in(own, 4), (number_of // 2,), 0, 1 << 20) % (slack + 1)
    tallies = tallies.at[source_of].add(-moved).at[taker].add(moved)
    members = jnp.searchsorted(jnp.cumsum(tallies), jnp.arange(rows * top), side="right").astype(jnp.int32)
    grid = members.reshape(top, rows).T
    grid = grid[jax.random.permutation(jax.random.fold_in(own, 1), rows)]
    turn = jax.random.randint(jax.random.fold_in(own, 2), (rows, 1), 0, top)
    return jnp.take_along_axis(grid, (jnp.arange(top)[None, :] + turn) % top, axis=1)


def shares(number_of, total, most, lean, full):
    loads = [(1 << 20) // math.isqrt(rank ** lean) + 1 for rank in range(1, number_of + 1)]
    largest = most if full else min(most, max(-(-total // number_of), total * loads[0] // sum(loads)))
    least = 1 if total - largest >= number_of - 1 else 0
    given, rest = [largest] + [least] * (number_of - 1), total - largest - least * (number_of - 1)
    while rest > 0:
        movable = [i for i in range(1, number_of) if given[i] < largest] or [i for i in range(1, number_of) if given[i] < most]
        whole, budget = sum([loads[i] for i in movable]), rest
        for i in movable:
            addition = min(most - given[i], max(1, budget * loads[i] // whole), rest)
            given[i] = given[i] + addition
            rest = rest - addition
    return np.array(given)


def noise(stream_key, shape, spread, most, cuts=(), kind=jnp.bfloat16):
    values = jax.random.normal(stream_key, shape, jnp.float32) * spread
    if len(cuts) > 0:
        values = levels(stream_key, shape, cuts, -0.22, 0.18) * values
    return jnp.clip(values, min=-most, max=most).astype(kind)


def setup_inputs(seed: int = 0) -> dict:
    arg_keys = jax.random.split(jax.random.key(seed), 14)
    tokens = noise(arg_keys[0], (TOKENS, D), 1.0, 6.0, ((0, 8),))
    cotangent = noise(arg_keys[1], (TOKENS, D), 1.0, 6.0, ((0, 8),))
    gain_attn = jnp.clip(1.0 + 0.18 * jax.random.normal(arg_keys[2], (D,), jnp.float32), 0.099609375, 1.8984375).astype(jnp.bfloat16)
    gain_ffn = jnp.clip(1.0 + 0.18 * jax.random.normal(arg_keys[3], (D,), jnp.float32), 0.099609375, 1.8984375).astype(jnp.bfloat16)
    w_qkv = noise(arg_keys[4], (3, D, HD), D ** -0.5, 0.21875, ((2, 4),))
    w_out = noise(arg_keys[5], (HD, D), (HD // 16) ** -0.5, 0.875, ((0, 4),))
    bias_table = noise(arg_keys[6], (NB, HEADS), 1.0, 4.0, ((1, 4),))
    router = noise(arg_keys[7], (D, EXPERTS), (2 * D) ** -0.5, 0.15625)
    w_in = noise(arg_keys[8], (EXPERTS, D, FF), D ** -0.5, 0.21875, ((0, 8), (2, 4)))
    w_down = noise(arg_keys[9], (EXPERTS, FF, D), FF ** -0.5, 0.109375, ((0, 8), (1, 4)))
    routes_keys = jax.random.split(jax.random.fold_in(arg_keys[10], 1), TOKENS // TOK_DEV)
    routes_turns = jax.random.permutation(jax.random.fold_in(arg_keys[10], 3), TOKENS // TOK_DEV)
    routes = jax.vmap(lambda own, number: shared_out(jax.random.fold_in(arg_keys[10], 2), own, number, TOK_DEV, EXPERTS, 2, CAP, 2))(routes_keys, routes_turns).reshape((TOKENS, 2))
    sequence_ids = draw_sequence_ids(jax.random.fold_in(arg_keys[13], 71), 0)
    rel_buckets = draw_rel_buckets(jax.random.fold_in(arg_keys[13], 71), 0)
    return dict(tokens=tokens, cotangent=cotangent, gain_attn=gain_attn, gain_ffn=gain_ffn, w_qkv=w_qkv, w_out=w_out, bias_table=bias_table, router=router, w_in=w_in, w_down=w_down, routes=routes, sequence_ids=sequence_ids, rel_buckets=rel_buckets)


EPSILON = 1e-06
PRECISE = lax.Precision.HIGHEST
FLOOR_SCORE = -1e+30

@jax.custom_vjp
def low(v):
    return lax.optimization_barrier(v.astype(jnp.bfloat16)).astype(jnp.float32)

@jax.custom_vjp
def low_back(v):
    return v

def low_keep(v):
    return (low(v), None)

def low_pass(kept, grad):
    return (grad,)

def back_keep(v):
    return (v, None)

def back_low(kept, grad):
    return (low(grad),)
low.defvjp(low_keep, low_pass)
low_back.defvjp(back_keep, back_low)

def rms_scale(values, gain_vec):
    inverse_rms = lax.rsqrt(lax.optimization_barrier(jnp.mean(values * values, axis=-1, keepdims=True)) + EPSILON)
    return values * inverse_rms * gain_vec

def attend_device(normed_rows, seq_ids, w_qkv, w_out, bias_table, rel_buckets):
    length = normed_rows.shape[0]
    projected = low(low_back(jnp.einsum('td,cdh->cth', normed_rows, w_qkv, precision=PRECISE)))
    split_heads = projected.reshape(3, length, HEADS, HK)
    scores = jnp.einsum('ihk,jhk->hij', split_heads[0], split_heads[1], precision=PRECISE) * HK ** (-0.5)
    positions = jnp.arange(length)
    distance = positions[:, None] - positions[None, :]
    bucket_grid = rel_buckets[jnp.clip(distance, 0, length - 1)]
    scores = low_back(scores + jnp.transpose(bias_table[bucket_grid], (2, 0, 1)))
    allowed = (distance >= 0) & (seq_ids[:, None] == seq_ids[None, :])
    scores = jnp.where(allowed[None], scores, FLOOR_SCORE)
    row_max = lax.optimization_barrier(jnp.max(scores, axis=-1, keepdims=True))
    exp_scores = jnp.exp(scores - row_max)
    probs_low = low(exp_scores / lax.optimization_barrier(jnp.sum(exp_scores, axis=-1, keepdims=True)))
    mixed_heads = jnp.einsum('hij,jhk->ihk', probs_low, split_heads[2], precision=PRECISE)
    mixed_flat = low(low_back(mixed_heads)).reshape(length, HEADS * HK)
    return low_back(jnp.dot(mixed_flat, w_out, precision=PRECISE))

def expert_slots(buffer_rows, w_in_one, w_down_one):
    share_width = w_in_one.shape[1] // N_TENSOR
    summed = jnp.zeros(buffer_rows.shape, buffer_rows.dtype)
    for lane_number in range(N_TENSOR):
        lo_col = lane_number * share_width
        lane_rows = low_back(buffer_rows)
        hidden_pre = low_back(jnp.dot(lane_rows, w_in_one[:, lo_col:lo_col + share_width], precision=PRECISE))
        hidden_act = low(jax.nn.gelu(hidden_pre))
        lane_part = jnp.dot(hidden_act, w_down_one[lo_col:lo_col + share_width], precision=PRECISE)
        summed = summed + low(low_back(lane_part))
    return summed

def layer_forward(inputs, gain_attn, gain_ffn, w_qkv, w_out, bias_table, router, w_in, w_down, routes, sequence_ids, rel_buckets):
    blocks = TOKENS // TOK_DEV
    normed_one = low(rms_scale(inputs, gain_attn))

    def attend_one(pair):
        return attend_device(pair[0], pair[1], w_qkv, w_out, bias_table, rel_buckets)
    attention = lax.map(jax.checkpoint(attend_one), (normed_one.reshape(blocks, TOK_DEV, D), sequence_ids.reshape(blocks, TOK_DEV)))
    middle = inputs + attention.reshape(TOKENS, D)
    normed_two = rms_scale(middle, gain_ffn)
    normed_low = low(normed_two)
    logits = jnp.dot(normed_two, router, precision=PRECISE)
    chosen = jnp.take_along_axis(logits, routes, axis=1)
    gate_values = jax.nn.softmax(chosen, axis=1)
    picks = routes.reshape(blocks, TOK_DEV * 2)
    marks = (picks[:, :, None] == jnp.arange(EXPERTS)[None, None, :]).astype(jnp.int32)
    rank_rows = lax.optimization_barrier(jnp.sum((jnp.cumsum(marks, axis=1) - 1) * marks, axis=2)).astype(jnp.int32)
    slot_index = (rank_rows + jnp.arange(blocks, dtype=jnp.int32)[:, None] * CAP).reshape(-1).astype(jnp.int32)
    flat_experts = routes.reshape(-1)
    token_index = jnp.arange(TOKENS * 2) // 2
    buffer_all = jnp.zeros((EXPERTS, N_EXPERT * CAP, D), inputs.dtype).at[flat_experts, slot_index].set(normed_low[token_index])

    def expert_one(triple):
        return expert_slots(triple[0], triple[1], triple[2])
    results = lax.map(jax.checkpoint(expert_one), (buffer_all, w_in, w_down))
    picked = results[flat_experts, slot_index].reshape(TOKENS, 2, D)
    expert_mix = lax.optimization_barrier(jnp.sum(gate_values[:, :, None] * picked, axis=1))
    return middle + expert_mix

def reference(tokens, cotangent, gain_attn, gain_ffn, w_qkv, w_out, bias_table, router, w_in, w_down, routes, sequence_ids, rel_buckets):
    floats = [array.astype(jnp.float32) for array in (tokens, gain_attn, gain_ffn, w_qkv, w_out, bias_table, router, w_in, w_down)]

    def forward_floats(inputs, gain_one, gain_two, qkv_f, out_f, table_f, router_f, in_f, down_f):
        return layer_forward(inputs, gain_one, gain_two, qkv_f, out_f, table_f, router_f, in_f, down_f, routes, sequence_ids, rel_buckets)
    output_rows, pullback = jax.vjp(forward_floats, *floats)
    grads = pullback(cotangent.astype(jnp.float32))
    return (output_rows.astype(jnp.bfloat16), grads[0].astype(jnp.bfloat16), grads[1], grads[2], grads[3], grads[4], grads[5], grads[6], grads[7], grads[8])
```

```python
import functools

import jax
import jax.numpy as jnp
from jax import lax
from jax.experimental import pallas as pl
from jax.experimental.pallas import tpu as pltpu
from jax.sharding import PartitionSpec as P

EPSILON = 1e-06
PRECISE = lax.Precision.HIGHEST
FLOOR_SCORE = -1e30
LOW = jnp.bfloat16
WIDE = jnp.float32
VMEM_BYTES = 56 * 1024 * 1024
QUERY_ROWS = 256


def dot_nn(left, right):
    return lax.dot_general(left, right, (((1,), (0,)), ((), ())), preferred_element_type=WIDE)


def dot_tn(left, right, precision=None):
    return lax.dot_general(
        left, right, (((0,), (0,)), ((), ())), precision=precision, preferred_element_type=WIDE
    )


def dot_nt(left, right, precision=None):
    return lax.dot_general(
        left, right, (((1,), (1,)), ((), ())), precision=precision, preferred_element_type=WIDE
    )


def normalize(values, gain_vec):
    scale_rows = lax.rsqrt(jnp.mean(values * values, axis=-1, keepdims=True) + EPSILON)
    plain_rows = values * scale_rows
    return (plain_rows, scale_rows, plain_rows * gain_vec)


def norm_back(grad_in, plain_rows, scale_rows, gain_vec):
    gain_grad = jnp.sum(grad_in * plain_rows, axis=0)
    inner_grad = grad_in * gain_vec
    spread_grad = scale_rows * (
        inner_grad - plain_rows * jnp.mean(inner_grad * plain_rows, axis=-1, keepdims=True)
    )
    return (spread_grad, gain_grad)


def head_lanes(width, head_size, head):
    lane = lax.broadcasted_iota(jnp.int32, (1, width), 1)
    return ((lane >= head * head_size) & (lane < (head + 1) * head_size)).astype(LOW)


def build_strips(lines_ref, strip_ref, heads, rows, length):
    for head in range(heads):
        line = jnp.broadcast_to(lines_ref[head : head + 1, :], (rows, length + rows))
        strip_ref[head] = pltpu.roll(line, 0, 1, stride=1, stride_axis=0)[:, :length]


def strip_scores(query, key, strip_ref, head, first, rows, width, length, col_ids, row_ids):
    scores = dot_nt(query, key) + strip_ref[head, :, length - width :]
    return jnp.where(col_ids == row_ids, scores, FLOOR_SCORE)


def attend_kernel(heads, head_size, rows, qkv_ref, lines_ref, ids_col, ids_row, o_ref, lse_ref, strip_ref):
    length, width_all = qkv_ref.shape[1:]
    build_strips(lines_ref, strip_ref, heads, rows, length)
    scale = head_size ** (-0.5)
    for first in range(0, length, rows):
        width = first + rows
        query = qkv_ref[0, first:width, :]
        key = qkv_ref[1, :width, :]
        value = qkv_ref[2, :width, :]
        mixed = jnp.zeros((rows, width_all), WIDE)
        for head in range(heads):
            lanes = head_lanes(width_all, head_size, head)
            scores = strip_scores(
                query * (lanes * LOW(scale)), key, strip_ref, head, first, rows, width, length,
                ids_col[first:width, :], ids_row[:, :width],
            )
            row_max = jnp.max(scores, axis=-1, keepdims=True)
            exp_scores = jnp.exp(scores - row_max)
            row_total = jnp.sum(exp_scores, axis=-1, keepdims=True)
            probs = (exp_scores * (1.0 / row_total)).astype(LOW)
            mixed = mixed + dot_nn(probs, value) * lanes.astype(WIDE)
            lse_ref[first:width, head : head + 1] = row_max + jnp.log(row_total)
        o_ref[first:width, :] = mixed.astype(LOW)


def attend_back_kernel(
    heads, head_size, rows, qkv_ref, do_ref, lse_ref, lines_ref, ids_col, ids_row,
    dqkv_ref, fold_ref, strip_ref, grad_strip, dk_acc, dv_acc,
):
    length, width_all = qkv_ref.shape[1:]
    build_strips(lines_ref, strip_ref, heads, rows, length)
    scale = head_size ** (-0.5)
    grad_strip[...] = jnp.zeros_like(grad_strip)
    dk_acc[...] = jnp.zeros_like(dk_acc)
    dv_acc[...] = jnp.zeros_like(dv_acc)
    for first in range(0, length, rows):
        width = first + rows
        query = qkv_ref[0, first:width, :]
        key = qkv_ref[1, :width, :]
        value = qkv_ref[2, :width, :]
        grad_out = do_ref[first:width, :]
        dq = jnp.zeros((rows, width_all), WIDE)
        for head in range(heads):
            lanes = head_lanes(width_all, head_size, head)
            query_head = query * (lanes * LOW(scale))
            grad_head = grad_out * lanes
            scores = strip_scores(
                query_head, key, strip_ref, head, first, rows, width, length,
                ids_col[first:width, :], ids_row[:, :width],
            )
            probs = jnp.exp(scores - lse_ref[first:width, head : head + 1])
            grad_probs = dot_nt(grad_head, value)
            inner = jnp.sum(probs * grad_probs, axis=-1, keepdims=True)
            grad_scores = (probs * (grad_probs - inner)).astype(LOW)
            grad_strip[head, :, length - width :] += grad_scores.astype(WIDE)
            dv_acc[:width, :] += dot_tn(probs.astype(LOW), grad_head)
            dk_acc[:width, :] += dot_tn(grad_scores, query_head)
            dq = dq + dot_nn(grad_scores, key) * lanes.astype(WIDE)
        dqkv_ref[0, first:width, :] = (dq * scale).astype(LOW)
    dqkv_ref[1] = dk_acc[...].astype(LOW)
    dqkv_ref[2] = dv_acc[...].astype(LOW)
    line_width = length + rows
    for head in range(heads):
        folded = jnp.concatenate(
            [grad_strip[head], jnp.zeros((rows, rows), WIDE)], axis=1
        )
        left = rows
        while left > 1:
            left //= 2
            folded = folded[:left] + pltpu.roll(folded[left:], line_width - left, 1)
        fold_ref[head : head + 1, :] = folded


def attend(qkv, lines, ids_col, ids_row, heads, head_size, rows):
    _, length, width = qkv.shape
    return pl.pallas_call(
        functools.partial(attend_kernel, heads, head_size, rows),
        out_shape=(
            jax.ShapeDtypeStruct((length, width), LOW),
            jax.ShapeDtypeStruct((length, heads), WIDE),
        ),
        scratch_shapes=[pltpu.VMEM((heads, rows, length), WIDE)],
        compiler_params=pltpu.CompilerParams(vmem_limit_bytes=VMEM_BYTES),
        name="attend",
    )(qkv, lines, ids_col, ids_row)


def attend_back(qkv, grad_out, lse, lines, ids_col, ids_row, heads, head_size, rows):
    _, length, width = qkv.shape
    return pl.pallas_call(
        functools.partial(attend_back_kernel, heads, head_size, rows),
        out_shape=(
            jax.ShapeDtypeStruct((3, length, width), LOW),
            jax.ShapeDtypeStruct((heads, length + rows), WIDE),
        ),
        scratch_shapes=[
            pltpu.VMEM((heads, rows, length), WIDE),
            pltpu.VMEM((heads, rows, length), WIDE),
            pltpu.VMEM((length, width), WIDE),
            pltpu.VMEM((length, width), WIDE),
        ],
        compiler_params=pltpu.CompilerParams(vmem_limit_bytes=VMEM_BYTES),
        name="attend_back",
    )(qkv, grad_out, lse, lines, ids_col, ids_row)


def swap(values, axis_name, bit):
    size = lax.axis_size(axis_name)
    return lax.ppermute(values, axis_name, [(i, i ^ bit) for i in range(size)])


def tensor_bits():
    size = lax.axis_size("tensor")
    return [1 << b for b in range(size.bit_length() - 1)]


def gather_tensor(values):
    blocks = {0: values}
    for bit in reversed(tensor_bits()):
        blocks.update({r | bit: swap(block, "tensor", bit) for r, block in blocks.items()})
    return [blocks[r] for r in range(len(blocks))]


def reduce_tensor(blocks):
    held = dict(enumerate(blocks))
    for bit in tensor_bits():
        sent = {r: block for r, block in held.items() if r & bit}
        held = {r: block for r, block in held.items() if not r & bit}
        for r, block in sent.items():
            arrived = swap(block.astype(LOW), "tensor", bit)
            held[r ^ bit] = held[r ^ bit].astype(WIDE) + arrived.astype(WIDE)
    return held[0]


def place_blocks(blocks):
    mine = lax.axis_index("tensor")
    rows = blocks[0].shape[0]
    whole = jnp.zeros((len(blocks) * rows,) + blocks[0].shape[1:], blocks[0].dtype)
    for r, block in enumerate(blocks):
        whole = lax.dynamic_update_slice_in_dim(whole, block, (mine ^ r) * rows, 0)
    return whole


def sum_small(values):
    for axis_name in ("tensor", "expert"):
        for b in range(lax.axis_size(axis_name).bit_length() - 1):
            values = values + swap(values, axis_name, 1 << b)
    return values


def line_pairs(size, move, held):
    return [(i, i + 2 * move) for i in range(size) if 0 <= i // 2 + move < size // 2 and held(i // 2)]


def side_pairs(size, held):
    return [(i, i ^ 1) for i in range(size) if held(i // 2)]


def gather_expert(values):
    size = lax.axis_size("expert")
    planes = size // 2
    plane = lax.axis_index("expert") // 2
    other = lax.ppermute(values, "expert", side_pairs(size, lambda p: True))
    up, down = [(values, other)], [(values, other)]
    for k in range(1, planes):
        above = lax.ppermute(up[-1][0], "expert", line_pairs(size, 1, lambda p: p >= k - 1))
        below = lax.ppermute(down[-1][0], "expert", line_pairs(size, -1, lambda p: p < planes - k + 1))
        up.append((above, lax.ppermute(above, "expert", side_pairs(size, lambda p: p >= k))))
        down.append((below, lax.ppermute(below, "expert", side_pairs(size, lambda p: p < planes - k))))
    blocks = [up[0]]
    for k in range(1, planes):
        blocks.append(tuple(jnp.where(plane >= k, up[k][s], down[planes - k][s]) for s in (0, 1)))
    return blocks


def reduce_expert(blocks):
    size = lax.axis_size("expert")
    planes = size // 2
    held = [
        near.astype(WIDE)
        + lax.ppermute(far, "expert", side_pairs(size, lambda p: True)).astype(WIDE)
        for near, far in blocks
    ]
    up = down = None
    for d in range(planes - 1, 0, -1):
        to_above = held[planes - d] if up is None else held[planes - d] + up
        to_below = held[d] if down is None else held[d] + down
        up = lax.ppermute(
            to_above.astype(LOW), "expert", line_pairs(size, 1, lambda p: p + d < planes)
        ).astype(WIDE)
        down = lax.ppermute(
            to_below.astype(LOW), "expert", line_pairs(size, -1, lambda p: p - d >= 0)
        ).astype(WIDE)
    return held[0] + up + down


def sum_expert(values):
    bits = [1 << b for b in range(lax.axis_size("expert").bit_length() - 1)]
    mine = lax.axis_index("expert")
    part = values
    for bit in bits:
        half = part.shape[0] // 2
        upper = (mine & bit) != 0
        keep = jnp.where(upper, part[half:], part[:half])
        give = jnp.where(upper, part[:half], part[half:])
        part = keep.astype(WIDE) + swap(give.astype(LOW), "expert", bit).astype(WIDE)
    part = part.astype(LOW)
    for bit in reversed(bits):
        other = swap(part, "expert", bit)
        upper = (mine & bit) != 0
        part = jnp.concatenate(
            [jnp.where(upper, other, part), jnp.where(upper, part, other)], axis=0
        )
    return part.astype(WIDE)


def dense_experts(normed_low, grad_low, gates, choose, routes, w_in, w_down):
    rows = normed_low.shape[0]
    size = lax.axis_size("expert")
    mine = lax.axis_index("expert")
    planes = size // 2
    order = jnp.stack(
        [
            ((mine // 2 - k) % planes) * 2 + ((mine % 2) ^ s)
            for k in range(planes)
            for s in (0, 1)
        ]
    )
    back_order = jnp.stack(
        [
            ((mine // 2 - source // 2) % planes) * 2 + ((mine % 2) ^ (source % 2))
            for source in range(size)
        ]
    )
    grad_rows = jnp.concatenate([b for pair in gather_expert(grad_low) for b in pair], axis=0)
    in_blocks = gather_tensor(w_in[0])
    down_blocks = gather_tensor(w_down[0])
    dense_gates = jnp.sum(gates[:, :, None] * choose, axis=1).T
    gate_rows = lax.all_to_all(dense_gates, "expert", split_axis=0, concat_axis=0, tiled=True)
    gate_rows = jnp.take(gate_rows, order, axis=0).reshape(size * rows, 1)
    token_rows = jnp.concatenate([b for pair in gather_expert(normed_low) for b in pair], axis=0)
    gated_grad = (gate_rows * grad_rows.astype(WIDE)).astype(LOW)
    expert_out = 0.0
    row_grad = 0.0
    in_grads = []
    down_grads = []
    for w_in_block, w_down_block in zip(in_blocks, down_blocks):
        hidden_pre = dot_nn(token_rows, w_in_block)
        hidden, gelu_back = jax.vjp(functools.partial(jax.nn.gelu, approximate=True), hidden_pre)
        hidden = hidden.astype(LOW)
        expert_out = expert_out + dot_nn(hidden, w_down_block).astype(LOW).astype(WIDE)
        grad_pre = gelu_back(dot_nt(gated_grad, w_down_block))[0].astype(LOW)
        row_grad = row_grad + dot_nt(grad_pre, w_in_block).astype(LOW).astype(WIDE)
        in_grads.append(dot_tn(token_rows, grad_pre))
        down_grads.append(dot_tn(hidden, gated_grad))

    def as_blocks(values):
        parts = values.reshape(planes, 2, rows, -1)
        return [(parts[k, 0], parts[k, 1]) for k in range(planes)]

    row_grad = reduce_expert(as_blocks(row_grad.astype(LOW)))
    mixed = reduce_expert(as_blocks((gate_rows * expert_out).astype(LOW)))
    gate_grad = jnp.sum(grad_rows.astype(WIDE) * expert_out, axis=1).reshape(size, rows)
    gate_grad = lax.all_to_all(
        jnp.take(gate_grad, back_order, axis=0), "expert", split_axis=0, concat_axis=0, tiled=True
    )
    gate_grad = jnp.sum(gate_grad.T[:, None, :] * choose, axis=-1)
    d_w_in = reduce_tensor(in_grads)[None]
    d_w_down = reduce_tensor(down_grads)[None]
    return mixed, gate_grad, row_grad, d_w_in, d_w_down


def pick_slots(buffer, flat_experts, slot_index, first_slot, slot_count):
    local_slot = slot_index - first_slot
    inside = ((local_slot >= 0) & (local_slot < slot_count)).astype(WIDE)
    rows = buffer[flat_experts, 0, jnp.clip(local_slot, 0, slot_count - 1)].astype(WIDE)
    return rows * inside[:, None]


def slot_experts(normed_low, grad_low, gates, choose, routes, w_in, w_down):
    own = normed_low.shape[0]
    tensor_size = lax.axis_size("tensor")
    sources = lax.axis_size("expert")
    first_own = lax.axis_index("tensor") * own
    length = own * tensor_size
    experts = choose.shape[2]
    model_width = normed_low.shape[1]
    capacity = 4 * length // experts
    share_rows = capacity // tensor_size
    first_share = lax.axis_index("tensor") * share_rows
    normed_all = lax.all_gather(normed_low, "tensor", axis=0, tiled=True)
    grad_all = lax.all_gather(grad_low, "tensor", axis=0, tiled=True)
    gates_all = lax.all_gather(gates, "tensor", axis=0, tiled=True)
    flat_experts = routes.reshape(-1)
    marks = (flat_experts[:, None] == jnp.arange(experts)[None, :]).astype(jnp.int32)
    slot_index = jnp.sum((jnp.cumsum(marks, axis=0) - 1) * marks, axis=1)
    token_index = jnp.arange(2 * length) // 2

    def send(values):
        empty = jnp.zeros((experts, 1, capacity, model_width), LOW)
        placed = empty.at[flat_experts, 0, slot_index].set(values)
        arrived = lax.all_to_all(placed, "expert", split_axis=0, concat_axis=1, tiled=True)
        return arrived.reshape(sources * capacity, model_width)

    def give_back(values):
        summed = lax.psum_scatter(
            values.reshape(sources, capacity, model_width), "tensor", scatter_dimension=1, tiled=True
        )
        returned = lax.all_to_all(
            summed.reshape(1, sources, share_rows, model_width),
            "expert", split_axis=1, concat_axis=0, tiled=True,
        )
        return pick_slots(returned, flat_experts, slot_index, first_share, share_rows).reshape(
            length, 2, model_width
        )

    expert_rows = send(normed_all[token_index])
    grad_wide = grad_all.astype(WIDE)
    toward = (gates_all[:, :, None] * grad_wide[:, None, :]).astype(LOW)
    grad_rows = send(toward.reshape(2 * length, model_width))
    hidden_pre = dot_nn(expert_rows, w_in[0])
    hidden, gelu_back = jax.vjp(functools.partial(jax.nn.gelu, approximate=True), hidden_pre)
    hidden = hidden.astype(LOW)
    picked = give_back(dot_nn(hidden, w_down[0]).astype(LOW))
    grad_pre = gelu_back(dot_nt(grad_rows, w_down[0]))[0].astype(LOW)
    d_w_down = dot_tn(hidden, grad_rows)[None]
    d_w_in = dot_tn(expert_rows, grad_pre)[None]
    back_rows = give_back(dot_nt(grad_pre, w_in[0]).astype(LOW))
    mixed = jnp.sum(gates_all[:, :, None] * picked, axis=1)
    gate_grad = jnp.sum(picked * grad_wide[:, None, :], axis=-1)
    mixed, gate_grad, row_grad = (
        lax.dynamic_slice_in_dim(values, first_own, own, 0)
        for values in lax.psum((mixed, gate_grad, jnp.sum(back_rows, axis=1)), "tensor")
    )
    return mixed, gate_grad, row_grad, d_w_in, d_w_down


def body(
    tokens,
    cotangent,
    gain_attn,
    gain_ffn,
    w_qkv,
    w_out,
    bias_table,
    router,
    w_in,
    w_down,
    routes,
    sequence_ids,
    rel_buckets,
):
    length, model_width = tokens.shape
    rows = min(QUERY_ROWS, length)
    bucket_count, heads = bias_table.shape
    width = w_qkv.shape[2]
    head_size = width // heads
    experts = router.shape[1]
    tensor_size = lax.axis_size("tensor")
    own = length // tensor_size
    mine = lax.axis_index("tensor")

    def own_rows(values):
        return lax.dynamic_slice_in_dim(values, mine * own, own, 0)

    gain_one = gain_attn.astype(WIDE)
    gain_two = gain_ffn.astype(WIDE)
    grad_low = own_rows(cotangent)
    grad_output = grad_low.astype(WIDE)
    own_inputs = own_rows(tokens).astype(WIDE)
    own_routes = own_rows(routes)
    out_blocks = gather_tensor(w_out)

    _, _, normed_one = normalize(tokens.astype(WIDE), gain_one)
    normed_low = normed_one.astype(LOW)
    qkv = jnp.einsum("td,cdh->cth", normed_low, w_qkv, preferred_element_type=WIDE).astype(LOW)
    line_width = length + rows
    place = jnp.arange(line_width)
    distance = jnp.where(place < length, length - rows - place, length - rows + line_width - place)
    buckets = rel_buckets[jnp.clip(distance, 0, length - 1)]
    bucket_pick = (
        (buckets[:, None] == jnp.arange(bucket_count)[None, :]) & (distance >= 0)[:, None]
    ).astype(WIDE)
    lines = dot_tn(bias_table.astype(WIDE), bucket_pick.T, PRECISE)
    lines = jnp.where((distance >= 0)[None, :], lines, FLOOR_SCORE)
    ids_col = sequence_ids[:, None]
    ids_row = sequence_ids[None, :]
    mixed_heads, lse = attend(qkv, lines, ids_col, ids_row, heads, head_size, rows)

    half = [mixed_heads]
    tags = [0]
    span = length
    for bit in reversed(tensor_bits()):
        span //= 2
        keep_at = jnp.where((mine & bit) != 0, span, 0)
        give_at = span - keep_at
        arrived = [
            swap(lax.dynamic_slice_in_dim(block, give_at, span, 0), "tensor", bit) for block in half
        ]
        half = [lax.dynamic_slice_in_dim(block, keep_at, span, 0) for block in half] + arrived
        tags = tags + [tag | bit for tag in tags]
    attention = sum(dot_nn(block, out_blocks[tag]) for tag, block in zip(tags, half))
    middle = own_inputs + attention
    plain_two, scale_two, normed_two = normalize(middle, gain_two)
    router_float = router.astype(WIDE)
    logits = jnp.dot(normed_two, router_float, precision=PRECISE)
    choose = (own_routes[:, :, None] == jnp.arange(experts)[None, None, :]).astype(WIDE)
    chosen = jnp.sum(logits[:, None, :] * choose, axis=-1)
    gates = jax.nn.softmax(chosen, axis=1)

    run_experts = dense_experts if lax.axis_size("expert") == 8 else slot_experts
    mixed, gate_grad, grad_normed_two, d_w_in, d_w_down = run_experts(
        normed_two.astype(LOW), grad_low, gates, choose, routes, w_in, w_down
    )
    output_rows = place_blocks(gather_tensor((middle + mixed).astype(LOW)))

    mean_grad = jnp.sum(gates * gate_grad, axis=1, keepdims=True)
    select_grad = gates * (gate_grad - mean_grad)
    logit_grad = jnp.sum(select_grad[:, :, None] * choose, axis=1)
    d_router = dot_tn(normed_two, logit_grad, PRECISE)
    grad_normed_two = grad_normed_two + dot_nt(logit_grad, router_float, PRECISE)
    back_two, d_gain_ffn = norm_back(grad_normed_two, plain_two, scale_two, gain_two)
    grad_middle = grad_output + back_two
    grad_attn = place_blocks(gather_tensor(grad_middle.astype(LOW)))
    d_out = sum_expert(dot_tn(mixed_heads, grad_attn))
    grad_mixed = dot_nt(grad_attn, w_out).astype(LOW)
    grad_qkv, fold = attend_back(
        qkv, grad_mixed, lse, lines, ids_col, ids_row, heads, head_size, rows
    )
    d_bias = dot_tn(bucket_pick, fold.T, PRECISE)
    d_qkv = sum_expert(
        jnp.concatenate([dot_tn(normed_low, grad_qkv[c]) for c in range(3)], axis=0)
    ).reshape(3, model_width, width)
    grad_one = sum(dot_nt(grad_qkv[c], w_qkv[c]) for c in range(3)).astype(LOW)
    grad_one = reduce_tensor(
        [lax.dynamic_slice_in_dim(grad_one, (mine ^ r) * own, own, 0) for r in range(tensor_size)]
    )
    plain_one, scale_one, _ = normalize(own_inputs, gain_one)
    back_one, d_gain_attn = norm_back(grad_one, plain_one, scale_one, gain_one)
    d_tokens = place_blocks(gather_tensor((grad_middle + back_one).astype(LOW)))

    bias_places = jnp.zeros((tensor_size, bucket_count * heads), WIDE)
    bias_places = lax.dynamic_update_slice_in_dim(bias_places, d_bias.reshape(1, -1), mine, 0)
    flat = jnp.concatenate(
        [d_gain_attn, d_gain_ffn, d_router.T.reshape(-1), bias_places.reshape(-1)]
    )
    pad = -flat.shape[0] % 1024
    flat = sum_small(jnp.pad(flat, (0, pad)).reshape(-1, 128)).reshape(-1)
    d_gain_attn = flat[:model_width]
    d_gain_ffn = flat[model_width : 2 * model_width]
    router_end = (2 + experts) * model_width
    d_router = flat[2 * model_width : router_end].reshape(experts, model_width).T
    bias_places = flat[router_end : router_end + bias_places.size].reshape(tensor_size, -1)
    d_bias = lax.dynamic_slice_in_dim(bias_places, mine, 1, 0).reshape(bucket_count, heads)
    return (
        output_rows,
        d_tokens,
        d_gain_attn,
        d_gain_ffn,
        d_qkv,
        d_out,
        d_bias,
        d_router,
        d_w_in,
        d_w_down,
    )


def solution(mesh):
    return jax.shard_map(
        body,
        mesh=mesh,
        in_specs=(
            P("expert", None),
            P("expert", None),
            P(),
            P(),
            P(None, None, "tensor"),
            P("tensor", None),
            P(None, "tensor"),
            P(),
            P("expert", None, "tensor"),
            P("expert", "tensor", None),
            P("expert", None),
            P("expert"),
            P(),
        ),
        out_specs=(
            P("expert", None),
            P("expert", None),
            P(),
            P(),
            P(None, None, "tensor"),
            P("tensor", None),
            P(None, "tensor"),
            P(),
            P("expert", None, "tensor"),
            P("expert", "tensor", None),
        ),
        check_vma=False,
    )
```

```python
import functools

import jax
import jax.numpy as jnp
from jax import lax
from jax.experimental import pallas as pl
from jax.experimental.pallas import tpu as pltpu
from jax.sharding import PartitionSpec as P

EPSILON = 1e-06
PRECISE = lax.Precision.HIGHEST
FLOOR_SCORE = -1e30
LOW = jnp.bfloat16
WIDE = jnp.float32
VMEM_BYTES = 62 * 1024 * 1024
QUERY_ROWS = 256


def dot_nn(left, right):
    return lax.dot_general(left, right, (((1,), (0,)), ((), ())), preferred_element_type=WIDE)


def dot_tn(left, right, precision=None):
    return lax.dot_general(
        left, right, (((0,), (0,)), ((), ())), precision=precision, preferred_element_type=WIDE
    )


def dot_nt(left, right, precision=None):
    return lax.dot_general(
        left, right, (((1,), (1,)), ((), ())), precision=precision, preferred_element_type=WIDE
    )


def dot_nn_precise(left, right):
    return jnp.dot(left, right, precision=PRECISE, preferred_element_type=WIDE)


def normalize(values, gain_vec):
    scale_rows = lax.rsqrt(jnp.mean(values * values, axis=-1, keepdims=True) + EPSILON)
    plain_rows = values * scale_rows
    return (plain_rows, scale_rows, plain_rows * gain_vec)


def norm_back(grad_in, plain_rows, scale_rows, gain_vec):
    gain_grad = jnp.sum(grad_in * plain_rows, axis=0)
    inner_grad = grad_in * gain_vec
    spread_grad = scale_rows * (
        inner_grad - plain_rows * jnp.mean(inner_grad * plain_rows, axis=-1, keepdims=True)
    )
    return (spread_grad, gain_grad)


def head_lanes(width, head_size, head):
    lane = lax.broadcasted_iota(jnp.int32, (1, width), 1)
    return ((lane >= head * head_size) & (lane < (head + 1) * head_size)).astype(LOW)


def build_strips(lines_ref, strip_ref, heads, rows, length):
    for head in range(heads):
        line = jnp.broadcast_to(lines_ref[head : head + 1, :], (rows, length + rows))
        strip_ref[head] = pltpu.roll(line, 0, 1, stride=1, stride_axis=0)[:, :length]


def strip_scores(query, key, strip_ref, head, first, rows, width, length, col_ids, row_ids):
    scores = dot_nt(query, key) + strip_ref[head, :, length - width :]
    return jnp.where(col_ids == row_ids, scores, FLOOR_SCORE)


def attend_kernel(heads, head_size, rows, qkv_ref, lines_ref, ids_col, ids_row, o_ref, lse_ref, strip_ref):
    length, width_all = qkv_ref.shape[1:]
    build_strips(lines_ref, strip_ref, heads, rows, length)
    scale = head_size ** (-0.5)
    for first in range(0, length, rows):
        width = first + rows
        query = qkv_ref[0, first:width, :]
        key = qkv_ref[1, :width, :]
        value = qkv_ref[2, :width, :]
        mixed = jnp.zeros((rows, width_all), WIDE)
        for head in range(heads):
            lanes = head_lanes(width_all, head_size, head)
            scores = strip_scores(
                query * (lanes * LOW(scale)), key, strip_ref, head, first, rows, width, length,
                ids_col[first:width, :], ids_row[:, :width],
            )
            row_max = jnp.max(scores, axis=-1, keepdims=True)
            exp_scores = jnp.exp(scores - row_max)
            row_total = jnp.sum(exp_scores, axis=-1, keepdims=True)
            probs = (exp_scores * (1.0 / row_total)).astype(LOW)
            mixed = mixed + dot_nn(probs, value) * lanes.astype(WIDE)
            lse_ref[first:width, head : head + 1] = row_max + jnp.log(row_total)
        o_ref[first:width, :] = mixed.astype(LOW)


def attend_back_kernel(
    heads, head_size, rows, tokens, qkv_ref, mixed_ref, grad_ref, normed_ref, w_qkv_ref, w_out_ref,
    lse_ref, lines_ref, ids_col, ids_row, *refs
):
    sums_ref, back_ref, fold_ref = refs[tokens : tokens + 3]
    strip_ref, grad_strip, do_ref, dqkv_ref, dk_acc, dv_acc = refs[tokens + 3 :]
    length, width_all = qkv_ref.shape[1:]
    model_width = normed_ref.shape[1]
    build_strips(lines_ref, strip_ref, heads, rows, length)
    scale = head_size ** (-0.5)
    grad_strip[...] = jnp.zeros_like(grad_strip)
    dk_acc[...] = jnp.zeros_like(dk_acc)
    dv_acc[...] = jnp.zeros_like(dv_acc)
    do_ref[...] = dot_nt(grad_ref[...], w_out_ref[...]).astype(LOW)
    sums_ref[3 * model_width :] = dot_tn(grad_ref[...], mixed_ref[...]).astype(LOW)
    for first in range(0, length, rows):
        width = first + rows
        query = qkv_ref[0, first:width, :]
        key = qkv_ref[1, :width, :]
        value = qkv_ref[2, :width, :]
        grad_out = do_ref[first:width, :]
        dq = jnp.zeros((rows, width_all), WIDE)
        for head in range(heads):
            lanes = head_lanes(width_all, head_size, head)
            query_head = query * (lanes * LOW(scale))
            grad_head = grad_out * lanes
            scores = strip_scores(
                query_head, key, strip_ref, head, first, rows, width, length,
                ids_col[first:width, :], ids_row[:, :width],
            )
            probs = jnp.exp(scores - lse_ref[first:width, head : head + 1])
            grad_probs = dot_nt(grad_head, value)
            inner = jnp.sum(probs * grad_probs, axis=-1, keepdims=True)
            grad_scores = (probs * (grad_probs - inner)).astype(LOW)
            grad_strip[head, :, length - width :] += grad_scores.astype(WIDE)
            dv_acc[:width, :] += dot_tn(probs.astype(LOW), grad_head)
            dk_acc[:width, :] += dot_tn(grad_scores, query_head)
            dq = dq + dot_nn(grad_scores, key) * lanes.astype(WIDE)
        dqkv_ref[0, first:width, :] = (dq * scale).astype(LOW)
    dqkv_ref[1] = dk_acc[...].astype(LOW)
    dqkv_ref[2] = dv_acc[...].astype(LOW)
    for c in range(3):
        sums_ref[c * model_width : (c + 1) * model_width] = dot_tn(
            normed_ref[...], dqkv_ref[c]
        ).astype(LOW)
    for first in range(0, length, rows):
        part = slice(first, first + rows)
        back = dot_nt(dqkv_ref[0, part], w_qkv_ref[0])
        for c in (1, 2):
            back = back + dot_nt(dqkv_ref[c, part], w_qkv_ref[c])
        back_ref[part] = back.astype(LOW)
    line_width = length + rows
    for head in range(heads):
        folded = jnp.concatenate(
            [grad_strip[head], jnp.zeros((rows, rows), WIDE)], axis=1
        )
        left = rows
        while left > 1:
            left //= 2
            folded = folded[:left] + pltpu.roll(folded[left:], line_width - left, 1)
        fold_ref[head : head + 1, :] = folded


def attend(qkv, lines, ids_col, ids_row, heads, head_size, rows):
    _, length, width = qkv.shape
    return pl.pallas_call(
        functools.partial(attend_kernel, heads, head_size, rows),
        out_shape=(
            jax.ShapeDtypeStruct((length, width), LOW),
            jax.ShapeDtypeStruct((length, heads), WIDE),
        ),
        scratch_shapes=[pltpu.VMEM((heads, rows, length), WIDE)],
        compiler_params=pltpu.CompilerParams(vmem_limit_bytes=VMEM_BYTES),
        cost_estimate=pl.CostEstimate(
            flops=200 * length * length * width, bytes_accessed=1 << 22, transcendentals=0
        ),
        name="attend",
    )(qkv, lines, ids_col, ids_row)


def attend_back(
    qkv, mixed, grad_attn, normed, w_qkv, w_out, lse, lines, ids_col, ids_row,
    heads, head_size, rows, tokens,
):
    _, length, width = qkv.shape
    model_width = normed.shape[1]
    operands = (qkv, mixed, grad_attn, normed, w_qkv, w_out, lse, lines, ids_col, ids_row)
    return pl.pallas_call(
        functools.partial(attend_back_kernel, heads, head_size, rows, len(tokens)),
        in_specs=[pl.BlockSpec(memory_space=pltpu.VMEM)] * len(operands) + [ANYWHERE] * len(tokens),
        out_shape=(
            jax.ShapeDtypeStruct((4 * model_width, width), LOW),
            jax.ShapeDtypeStruct((length, model_width), LOW),
            jax.ShapeDtypeStruct((heads, length + rows), WIDE),
        ),
        scratch_shapes=[
            pltpu.VMEM((heads, rows, length), WIDE),
            pltpu.VMEM((heads, rows, length), WIDE),
            pltpu.VMEM((length, width), LOW),
            pltpu.VMEM((3, length, width), LOW),
            pltpu.VMEM((length, width), WIDE),
            pltpu.VMEM((length, width), WIDE),
        ],
        compiler_params=pltpu.CompilerParams(vmem_limit_bytes=VMEM_BYTES),
        cost_estimate=pl.CostEstimate(
            flops=200 * length * length * width, bytes_accessed=1 << 22, transcendentals=0
        ),
        name="attend_back",
    )(*operands, *tokens)


ANYWHERE = pl.BlockSpec(memory_space=pltpu.HBM)


def tie(values, *earlier):
    def kernel(*refs):
        pass

    return pl.pallas_call(
        kernel,
        out_shape=jax.ShapeDtypeStruct(values.shape, values.dtype),
        in_specs=[ANYWHERE] * (1 + len(earlier)),
        out_specs=ANYWHERE,
        input_output_aliases={0: 0},
        name="tie",
    )(values, *earlier)


def swap(values, axis_name, bit):
    size = lax.axis_size(axis_name)
    return lax.ppermute(values, axis_name, [(i, i ^ bit) for i in range(size)])


def tensor_bits():
    size = lax.axis_size("tensor")
    return [1 << b for b in range(size.bit_length() - 1)]


def gather_tensor(values):
    blocks = {0: values}
    for bit in reversed(tensor_bits()):
        blocks.update({r | bit: swap(block, "tensor", bit) for r, block in blocks.items()})
    return [blocks[r] for r in range(len(blocks))]


def place_blocks(blocks):
    rows = blocks[0].shape[0]
    count = len(blocks)

    def kernel(mine, *refs):
        for r in range(count):
            first = pl.multiple_of((mine[0] ^ r) * rows, rows)
            refs[count][pl.ds(first, rows)] = refs[r][...]

    return pl.pallas_call(
        kernel,
        out_shape=jax.ShapeDtypeStruct((count * rows,) + blocks[0].shape[1:], blocks[0].dtype),
        in_specs=[pl.BlockSpec(memory_space=pltpu.SMEM)]
        + [pl.BlockSpec(memory_space=pltpu.VMEM)] * count,
        out_specs=pl.BlockSpec(memory_space=pltpu.VMEM),
        name="place",
    )(lax.axis_index("tensor").astype(jnp.int32).reshape(1), *blocks)


def sum_small(values):
    for axis_name in ("tensor", "expert"):
        for b in range(lax.axis_size(axis_name).bit_length() - 1):
            values = values + swap(values, axis_name, 1 << b)
    return values


def sum_expert(values, beside):
    size = lax.axis_size("expert")
    parts = values.astype(LOW).reshape((size, values.shape[0] // size) + values.shape[1:])
    parts = tie(lax.all_to_all(parts, "expert", split_axis=0, concat_axis=0, tiled=True), beside)
    part = jnp.sum(parts.astype(WIDE), axis=0).astype(LOW)
    parts = jnp.broadcast_to(part[None], parts.shape)
    parts = lax.all_to_all(parts, "expert", split_axis=0, concat_axis=0, tiled=True)
    return parts.reshape(values.shape).astype(WIDE)


def pick_rows(near, far, chosen):
    rows = near.shape[0]
    return dot_nn(chosen[:, :rows], near) + dot_nn(chosen[:, rows:], far)


def gelu_pair(values):
    slope = (2.0 / jnp.pi) ** 0.5
    square = values * values
    bend = jnp.tanh(slope * values * (1.0 + 0.044715 * square))
    outer = 0.5 + 0.5 * bend
    steep = slope * (1.0 + 3 * 0.044715 * square)
    return values * outer, outer + 0.5 * values * (1.0 - bend * bend) * steep


def short_rows(rows):
    return rows * 9 // 16 // 16 * 16


def split_low(values, rounded=lambda values: values.astype(LOW).astype(WIDE)):
    pieces = []
    for _ in range(3):
        piece = rounded(values)
        pieces.append(piece.astype(LOW))
        values = values - piece
    return pieces


def round_low(values):
    return lax.reduce_precision(values, 8, 7)


def expert_kernel(blocks, chunk, experts, tokens, joined, meta, near, far, grads, *refs):
    weights, refs = refs[: 2 * blocks], refs[2 * blocks + tokens :]
    (kept_rows, kept_grads, count, hidden_out, pre_out), refs = refs[:5], refs[5:]
    if joined:
        backs, refs = refs[:2], refs[2:]
        mix_outs = None
    else:
        backs, mix_outs, refs = refs[:2], refs[2:4], refs[4:]
    weight_buf, grad_buf, hidden_buf, pre_buf, weight_sem, grad_sem, out_sem = refs
    span = grad_buf.shape[0]
    rows = span // 2
    model_width = near.shape[1]
    mine = meta[0]

    def weight_copy(n):
        return pltpu.make_async_copy(weights[n], weight_buf.at[n], weight_sem.at[n])

    def side_rows(side):
        return pl.ds(pl.multiple_of((mine ^ (2 * chunk + side)) * rows, rows), rows)

    def grad_copy(side):
        return pltpu.make_async_copy(
            grads.at[side_rows(side)], grad_buf.at[pl.ds(side * rows, rows)], grad_sem.at[side]
        )

    for side in (0, 1):
        grad_copy(side).start()
    for n in range(2 * blocks):
        weight_copy(n).start()

    def gates_of(payload):
        extra = payload[rows : rows + experts, :].astype(WIDE)
        here = lax.broadcasted_iota(jnp.int32, extra.shape, 0) == mine
        line = jnp.sum(jnp.where(here, extra, 0.0), axis=0, keepdims=True)
        return line[:, :rows] + line[:, rows : 2 * rows] + line[:, 2 * rows :]

    gate_row = jnp.concatenate([gates_of(near), gates_of(far)], axis=1)
    routed = gate_row != 0.0
    earlier = lax.broadcasted_iota(jnp.int32, (span, span), 0) < lax.broadcasted_iota(
        jnp.int32, (span, span), 1
    )
    routed_wide = routed.astype(WIDE)
    rank = dot_nn(
        jnp.broadcast_to(routed_wide, (8, span)).astype(LOW), earlier.astype(WIDE).astype(LOW)
    )[:1]
    rank = jnp.where(routed, rank, -1.0).astype(jnp.int32)
    total = jnp.sum(routed_wide).astype(jnp.int32)
    count[0] = total

    def run(taken):
        def out_copy(n, buffer, target, lane):
            return pltpu.make_async_copy(
                buffer.at[n, pl.ds(0, taken)], target.at[n, pl.ds(0, taken)], out_sem.at[lane, n]
            )

        chosen_wide = (rank == lax.broadcasted_iota(jnp.int32, (taken, span), 0)).astype(WIDE)
        chosen = chosen_wide.astype(LOW)
        picked = pick_rows(near[:rows], far[:rows], chosen).astype(LOW)
        gate_col = jnp.sum(chosen_wide * gate_row, axis=1, keepdims=True)
        for side in (0, 1):
            grad_copy(side).wait()
        grad_rows = pick_rows(grad_buf[:rows], grad_buf[rows:], chosen)
        gated = (gate_col * grad_rows).astype(LOW)
        kept_rows[:taken] = picked
        kept_grads[:taken] = gated
        expert_out = jnp.zeros((taken, model_width), WIDE)
        row_grad = jnp.zeros((taken, model_width), WIDE)
        for n in range(blocks):
            w_in, w_down = weight_buf.at[2 * n], weight_buf.at[2 * n + 1]
            weight_copy(2 * n).wait()
            weight_copy(2 * n + 1).wait()
            value, slope = gelu_pair(dot_nn(picked, w_in[...]))
            hidden = value.astype(LOW)
            hidden_buf[n, :taken] = hidden
            out_copy(n, hidden_buf, hidden_out, 0).start()
            pre_grad = (dot_nt(gated, w_down[...]) * slope).astype(LOW)
            pre_buf[n, :taken] = pre_grad
            out_copy(n, pre_buf, pre_out, 1).start()
            expert_out = expert_out + dot_nn(hidden, w_down[...]).astype(LOW).astype(WIDE)
            row_grad = row_grad + dot_nt(pre_grad, w_in[...]).astype(LOW).astype(WIDE)
        mixed = dot_tn(chosen, (gate_col * expert_out).astype(LOW)).astype(LOW)
        back = dot_tn(chosen, row_grad.astype(LOW)).astype(LOW)
        grad_col = jnp.sum(grad_rows * expert_out, axis=1, keepdims=True)
        gate_grad = jnp.sum(chosen_wide * grad_col, axis=0, keepdims=True)
        extra = payload_rows(rows, experts) - rows
        for side, back_out in enumerate(backs):
            part = slice(side * rows, (side + 1) * rows)
            back_out[:rows] = back[part]
            pieces = split_low(gate_grad[:, part])
            line = jnp.concatenate([piece.astype(WIDE) for piece in pieces], axis=1)
            here = lax.broadcasted_iota(jnp.int32, (extra, model_width), 0) == mine
            back_out[rows : rows + extra] = jnp.where(here, line, 0.0).astype(LOW)
            if joined:
                back_out[rows + extra :] = mixed[part]
            else:
                mix_outs[side][...] = mixed[part]
        for n in range(blocks):
            out_copy(n, hidden_buf, hidden_out, 0).wait()
            out_copy(n, pre_buf, pre_out, 1).wait()

    few = total <= short_rows(span)

    @pl.when(few)
    def _():
        run(short_rows(span))

    @pl.when(jnp.logical_not(few))
    def _():
        run(span)


def payload_rows(rows, experts):
    return rows + -(-experts // 16) * 16


def expert_chunk(chunk, experts, rows, joined, meta, near, far, grads, weights, tokens):
    payload, model_width = near.shape
    span = 2 * rows
    blocks = len(weights) // 2
    block_width = weights[0].shape[1]
    low = functools.partial(jax.ShapeDtypeStruct, dtype=LOW)
    vmem = pl.BlockSpec(memory_space=pltpu.VMEM)
    smem = pl.BlockSpec(memory_space=pltpu.SMEM)
    sides = [low((payload + rows, model_width))] * 2
    if not joined:
        sides = [low((payload, model_width))] * 2 + [low((rows, model_width))] * 2
    return pl.pallas_call(
        functools.partial(expert_kernel, blocks, chunk, experts, len(tokens), joined),
        out_shape=(
            low((span, model_width)),
            low((span, model_width)),
            jax.ShapeDtypeStruct((1,), jnp.int32),
            low((blocks, span, block_width)),
            low((blocks, span, block_width)),
            *sides,
        ),
        in_specs=[smem, vmem, vmem] + [ANYWHERE] * (1 + len(weights) + len(tokens)),
        out_specs=(vmem, vmem, smem, ANYWHERE, ANYWHERE) + (vmem,) * len(sides),
        scratch_shapes=[
            pltpu.VMEM((2 * blocks,) + weights[0].shape, LOW),
            pltpu.VMEM((span, model_width), LOW),
            pltpu.VMEM((blocks, span, block_width), LOW),
            pltpu.VMEM((blocks, span, block_width), LOW),
            pltpu.SemaphoreType.DMA((2 * blocks,)),
            pltpu.SemaphoreType.DMA((2,)),
            pltpu.SemaphoreType.DMA((2, blocks)),
        ],
        compiler_params=pltpu.CompilerParams(vmem_limit_bytes=VMEM_BYTES),
        cost_estimate=pl.CostEstimate(
            flops=200 * short_rows(span) * model_width * block_width * blocks,
            bytes_accessed=1 << 24,
            transcendentals=0,
        ),
        name="expert_chunk",
    )(meta, near, far, grads, *weights, *tokens)


def weight_grad_kernel(chunks, block, tokens, *refs):
    counts, refs = refs[:chunks], refs[chunks:]
    kept, refs = refs[: 4 * chunks], refs[4 * chunks + tokens :]
    done, refs = refs[0], refs[1:]
    done[0] = counts[0][0]
    if block:
        out_ref, refs = refs[0], refs[1:]
    in_grad, down_grad, row_buf, grad_buf, hidden_buf, pre_buf, sem = refs
    span = row_buf.shape[1]

    def by_count(chunk, action):
        few = counts[chunk][0] <= short_rows(span)

        @pl.when(few)
        def _():
            action(short_rows(span))

        @pl.when(jnp.logical_not(few))
        def _():
            action(span)

    def copies(chunk, taken):
        rows, grads, hidden, pre = kept[4 * chunk : 4 * chunk + 4]
        part = pl.ds(0, taken)
        return [
            pltpu.make_async_copy(source, target, sem.at[chunk, n])
            for n, (source, target) in enumerate(
                (
                    (rows.at[part], row_buf.at[chunk, part]),
                    (grads.at[part], grad_buf.at[chunk, part]),
                    (hidden.at[block, part], hidden_buf.at[chunk, part]),
                    (pre.at[block, part], pre_buf.at[chunk, part]),
                )
            )
        ]

    for chunk in range(chunks):
        by_count(chunk, lambda taken, chunk=chunk: [copy.start() for copy in copies(chunk, taken)])

    def add(chunk, taken):
        for copy in copies(chunk, taken):
            copy.wait()
        in_part = dot_tn(row_buf[chunk, :taken], pre_buf[chunk, :taken])
        down_part = dot_tn(hidden_buf[chunk, :taken], grad_buf[chunk, :taken])
        if chunk == 0:
            in_grad[...] = in_part
            down_grad[...] = down_part
        elif chunk == chunks - 1 and block:
            out_ref[0] = (in_grad[...] + in_part).astype(LOW)
            out_ref[1] = (down_grad[...] + down_part).astype(LOW)
        else:
            in_grad[...] += in_part
            down_grad[...] += down_part

    for chunk in range(chunks):
        by_count(chunk, functools.partial(add, chunk))


def weight_grads(block, counts, kept, tokens):
    chunks = len(kept)
    span, model_width = kept[0][0].shape
    block_width = kept[0][2].shape[2]
    accumulators = [(model_width, block_width), (block_width, model_width)]
    if block:
        out_shape = (jax.ShapeDtypeStruct((2, model_width, block_width), LOW),)
        extra = [pltpu.VMEM(shape, WIDE) for shape in accumulators]
    else:
        out_shape = tuple(jax.ShapeDtypeStruct(shape, WIDE) for shape in accumulators)
        extra = []
    return pl.pallas_call(
        functools.partial(weight_grad_kernel, chunks, block, len(tokens)),
        out_shape=(jax.ShapeDtypeStruct((1,), jnp.int32),) + out_shape,
        out_specs=(pl.BlockSpec(memory_space=pltpu.SMEM),)
        + (pl.BlockSpec(memory_space=pltpu.VMEM),) * len(out_shape),
        in_specs=[pl.BlockSpec(memory_space=pltpu.SMEM)] * chunks
        + [ANYWHERE] * (4 * chunks + len(tokens)),
        scratch_shapes=extra
        + [
            pltpu.VMEM((chunks, span, model_width), LOW),
            pltpu.VMEM((chunks, span, model_width), LOW),
            pltpu.VMEM((chunks, span, block_width), LOW),
            pltpu.VMEM((chunks, span, block_width), LOW),
            pltpu.SemaphoreType.DMA((chunks, 4)),
        ],
        compiler_params=pltpu.CompilerParams(vmem_limit_bytes=VMEM_BYTES),
        cost_estimate=pl.CostEstimate(
            flops=120 * chunks * short_rows(span) * model_width * block_width,
            bytes_accessed=1 << 23,
            transcendentals=0,
        ),
        name="weight_grads",
    )(*counts, *[array for four in kept for array in four], *tokens)


def dense_experts(normed_low, grad_low, gates, choose, routes, gathered):
    rows, model_width = normed_low.shape
    experts = choose.shape[2]
    size = lax.axis_size("expert")
    chunks = size // 2
    meta = lax.axis_index("expert").astype(jnp.int32).reshape(1)
    w_in_blocks, w_down_own, w_down_far, grad_all = gathered
    dense_gates = jnp.sum(gates[:, :, None] * choose, axis=1).T
    gate_rows = jnp.concatenate(split_low(dense_gates, round_low), axis=1)
    payload = jnp.concatenate([normed_low, gate_rows], axis=0)
    payload = jnp.pad(payload, ((0, payload_rows(rows, experts) - payload.shape[0]), (0, 0)))
    run = functools.partial(expert_chunk, rows=rows, experts=experts, meta=meta, grads=grad_all)

    def side_swap(values):
        return swap(values, "expert", 1)

    def plane_swap(chunk, values):
        return swap(values, "expert", 2 * chunk)

    far = [side_swap(payload)]
    near = [payload, plane_swap(1, payload)]
    near[1] = tie(near[1], far[0])
    far.append(side_swap(near[1]))
    near.append(plane_swap(2, tie(payload, near[1])))
    last_down = tie(w_down_far, near[1])
    in_blocks = w_in_blocks
    down_blocks = [w_down_own, swap(w_down_own, "tensor", 1), last_down, swap(last_down, "tensor", 1)]
    weights = [block for pair in zip(in_blocks, down_blocks) for block in pair]

    kept, counts, held, flown, mixes, backs = [], [], [], [], [], []

    def chunk_step(chunk, tokens):
        joined = chunk < 2
        rows_c, grads_c, count, hidden, pre, back_near, back_far, *mixed = run(
            chunk, joined=joined, near=near[chunk], far=far[chunk], weights=weights, tokens=tokens
        )
        kept.append((rows_c, grads_c, hidden, pre))
        counts.append(count)
        mixes.append(mixed)
        backs.append((back_near, side_swap(back_far)))

    def hold(chunk, token):
        back_near, arrived = backs[chunk]
        return (back_near.astype(WIDE) + tie(arrived, token).astype(WIDE)).astype(LOW)

    chunk_step(0, [])
    near[2] = tie(near[2], counts[0])
    far.append(side_swap(near[2]))
    near.append(plane_swap(3, tie(payload, near[2])))
    chunk_step(1, [counts[0]])
    near[3] = tie(near[3], counts[1])
    far.append(side_swap(near[3]))
    held.append(hold(0, counts[1]))
    chunk_step(2, [counts[1], held[0]])
    held.append(hold(1, counts[2]))
    flown.append(plane_swap(1, held[1]))
    chunk_step(3, [counts[2], held[1]])
    held.append(hold(2, counts[3]))
    flown[0] = tie(flown[0], counts[3])
    flown.append(plane_swap(2, held[2]))
    joint = held[0].astype(WIDE) + flown[0].astype(WIDE)
    grads_of = functools.partial(weight_grads, counts=counts, kept=kept)
    done3, block3 = grads_of(3, tokens=[flown[0], held[2]])
    held.append(hold(3, done3))
    flown.append(plane_swap(3, held[3]))
    core3 = swap(block3, "tensor", 1)
    late = [side_swap(tie(mixes[chunk][1], held[3])) for chunk in (2, 3)]
    done2, block2 = grads_of(2, tokens=[done3, held[3]])
    flown[1] = tie(flown[1], done2)
    flown[2] = tie(flown[2], done2)
    chip_sum = (block2.astype(WIDE) + tie(core3, done2).astype(WIDE)).astype(LOW)
    late = [
        (mixes[chunk][0].astype(WIDE) + tie(arrived, done2).astype(WIDE)).astype(LOW)
        for chunk, arrived in zip((2, 3), late)
    ]
    late = [plane_swap(chunk, values) for chunk, values in zip((2, 3), late)]
    payload = payload.shape[0]
    row_grad = joint[:payload] + flown[1].astype(WIDE) + flown[2].astype(WIDE)
    tail = row_grad[rows : rows + experts]
    gate_grad = tail[:, :rows] + tail[:, rows : 2 * rows] + tail[:, 2 * rows :]
    gate_grad = jnp.sum(gate_grad.T[:, None, :] * choose, axis=-1)

    def early_weights(token):
        return grads_of(1, tokens=[token])

    def send_weights(n, arrived):
        sent = chip_sum[n] if arrived is None else tie(chip_sum[n], arrived)
        return swap(sent, "tensor", 2)

    def finish_mixed(token):
        mixed = joint[payload:]
        for values in late:
            mixed = mixed + tie(values, token).astype(WIDE)
        return mixed

    def finish_weights(block1, token):
        done0, *block0 = grads_of(0, tokens=[token])
        near_sum = tie(swap(block1, "tensor", 1), token)
        return done0, lambda far_sums: tuple(
            (block0[n] + near_sum[n].astype(WIDE) + far_sums[n].astype(WIDE))[None] for n in (0, 1)
        )

    return gate_grad, row_grad[:rows], early_weights, send_weights, finish_mixed, finish_weights


def pick_slots(buffer, flat_experts, slot_index, first_slot, slot_count):
    local_slot = slot_index - first_slot
    inside = ((local_slot >= 0) & (local_slot < slot_count)).astype(WIDE)
    rows = buffer[flat_experts, 0, jnp.clip(local_slot, 0, slot_count - 1)].astype(WIDE)
    return rows * inside[:, None]


def slot_experts(normed_low, grad_low, gates, choose, routes, gathered):
    w_in, w_down = gathered
    own = normed_low.shape[0]
    tensor_size = lax.axis_size("tensor")
    sources = lax.axis_size("expert")
    first_own = lax.axis_index("tensor") * own
    length = own * tensor_size
    experts = choose.shape[2]
    model_width = normed_low.shape[1]
    capacity = 4 * length // experts
    share_rows = capacity // tensor_size
    first_share = lax.axis_index("tensor") * share_rows
    normed_all = lax.all_gather(normed_low, "tensor", axis=0, tiled=True)
    grad_all = lax.all_gather(grad_low, "tensor", axis=0, tiled=True)
    gates_all = lax.all_gather(gates, "tensor", axis=0, tiled=True)
    flat_experts = routes.reshape(-1)
    marks = (flat_experts[:, None] == jnp.arange(experts)[None, :]).astype(jnp.int32)
    slot_index = jnp.sum((jnp.cumsum(marks, axis=0) - 1) * marks, axis=1)
    token_index = jnp.arange(2 * length) // 2

    def send(values):
        empty = jnp.zeros((experts, 1, capacity, model_width), LOW)
        placed = empty.at[flat_experts, 0, slot_index].set(values)
        arrived = lax.all_to_all(placed, "expert", split_axis=0, concat_axis=1, tiled=True)
        return arrived.reshape(sources * capacity, model_width)

    def give_back(values):
        summed = lax.psum_scatter(
            values.reshape(sources, capacity, model_width), "tensor", scatter_dimension=1, tiled=True
        )
        returned = lax.all_to_all(
            summed.reshape(1, sources, share_rows, model_width),
            "expert", split_axis=1, concat_axis=0, tiled=True,
        )
        return pick_slots(returned, flat_experts, slot_index, first_share, share_rows).reshape(
            length, 2, model_width
        )

    expert_rows = send(normed_all[token_index])
    grad_wide = grad_all.astype(WIDE)
    toward = (gates_all[:, :, None] * grad_wide[:, None, :]).astype(LOW)
    grad_rows = send(toward.reshape(2 * length, model_width))
    hidden_pre = dot_nn(expert_rows, w_in[0])
    hidden, gelu_back = jax.vjp(functools.partial(jax.nn.gelu, approximate=True), hidden_pre)
    hidden = hidden.astype(LOW)
    picked = give_back(dot_nn(hidden, w_down[0]).astype(LOW))
    grad_pre = gelu_back(dot_nt(grad_rows, w_down[0]))[0].astype(LOW)
    d_w_down = dot_tn(hidden, grad_rows)[None]
    d_w_in = dot_tn(expert_rows, grad_pre)[None]
    back_rows = give_back(dot_nt(grad_pre, w_in[0]).astype(LOW))
    mixed = jnp.sum(gates_all[:, :, None] * picked, axis=1)
    gate_grad = jnp.sum(picked * grad_wide[:, None, :], axis=-1)
    mixed, gate_grad, row_grad = (
        lax.dynamic_slice_in_dim(values, first_own, own, 0)
        for values in lax.psum((mixed, gate_grad, jnp.sum(back_rows, axis=1)), "tensor")
    )
    token = gate_grad[:1, :1]
    return (
        gate_grad,
        row_grad,
        lambda token: (token, token),
        lambda n, arrived: token,
        lambda token: mixed,
        lambda block1, token: (token, lambda far_sums: (d_w_in, d_w_down)),
    )


def body(
    tokens,
    cotangent,
    gain_attn,
    gain_ffn,
    w_qkv,
    w_out,
    bias_table,
    router,
    w_in,
    w_down,
    routes,
    sequence_ids,
    rel_buckets,
):
    length, model_width = tokens.shape
    rows = min(QUERY_ROWS, length)
    bucket_count, heads = bias_table.shape
    width = w_qkv.shape[2]
    head_size = width // heads
    experts = router.shape[1]
    tensor_size = lax.axis_size("tensor")
    own = length // tensor_size
    mine = lax.axis_index("tensor")

    def own_rows(values):
        return lax.dynamic_slice_in_dim(values, mine * own, own, 0)

    gain_one = gain_attn.astype(WIDE)
    gain_two = gain_ffn.astype(WIDE)
    grad_low = own_rows(cotangent)
    grad_output = grad_low.astype(WIDE)
    own_inputs = own_rows(tokens).astype(WIDE)
    own_routes = own_rows(routes)
    out_blocks = gather_tensor(w_out)

    _, _, normed_one = normalize(tokens.astype(WIDE), gain_one)
    normed_low = normed_one.astype(LOW)
    qkv = jnp.einsum("td,cdh->cth", normed_low, w_qkv, preferred_element_type=WIDE).astype(LOW)
    line_width = length + rows
    place = jnp.arange(line_width)
    distance = jnp.where(place < length, length - rows - place, 2 * length - place)
    buckets = jnp.concatenate(
        [
            rel_buckets[: length - rows + 1][::-1],
            jnp.zeros((rows,), jnp.int32),
            rel_buckets[length - rows + 1 :][::-1],
        ]
    )
    bucket_pick = (
        (buckets[:, None] == jnp.arange(bucket_count)[None, :]) & (distance >= 0)[:, None]
    ).astype(WIDE)
    lines = dot_tn(bias_table.astype(WIDE), bucket_pick.T, PRECISE)
    lines = jnp.where((distance >= 0)[None, :], lines, FLOOR_SCORE)
    ids_col = sequence_ids[:, None]
    ids_row = sequence_ids[None, :]
    mixed_heads, lse = attend(qkv, lines, ids_col, ids_row, heads, head_size, rows)

    whole_width = (
        lax.axis_size("expert") == 8
        and tensor_size == 4
        and 3 * own == model_width
        and w_in.shape[2] == model_width
    )
    if whole_width:
        w_in_far = tie(swap(w_in[0], "tensor", 2), lse)
        w_in_near = swap(w_in[0], "tensor", 1)

    half = [mixed_heads]
    tags = [0]
    span = length
    for bit in reversed(tensor_bits()):
        span //= 2
        keep_at = jnp.where((mine & bit) != 0, span, 0)
        give_at = span - keep_at
        given = [lax.dynamic_slice_in_dim(block, give_at, span, 0) for block in half]
        if whole_width and len(half) == 1:
            given = [tie(given[0], w_in_far)]
        arrived = [swap(block, "tensor", bit) for block in given]
        half = [lax.dynamic_slice_in_dim(block, keep_at, span, 0) for block in half] + arrived
        tags = tags + [tag | bit for tag in tags]
    attention = sum(dot_nn(block, out_blocks[tag]) for tag, block in zip(tags, half))
    middle = own_inputs + attention
    plain_two, scale_two, normed_two = normalize(middle, gain_two)
    router_float = router.astype(WIDE)
    logits = jnp.dot(normed_two, router_float, precision=PRECISE)
    choose = (own_routes[:, :, None] == jnp.arange(experts)[None, None, :]).astype(WIDE)
    chosen = jnp.sum(logits[:, None, :] * choose, axis=-1)
    gates = jax.nn.softmax(chosen, axis=1)

    if whole_width:
        w_down_own = tie(w_down[0], half[1])
        gathered = (
            [w_in[0], w_in_near, w_in_far, swap(w_in_far, "tensor", 1)],
            w_down_own,
            swap(w_down_own, "tensor", 2),
            lax.all_gather(grad_low, "expert", axis=0, tiled=True),
        )
    else:
        gathered = (w_in, w_down)
    run_experts = dense_experts if whole_width else slot_experts
    gate_grad, grad_normed_two, early_weights, send_weights, finish_mixed, finish_weights = run_experts(
        normed_two.astype(LOW), grad_low, gates, choose, routes, gathered
    )

    mean_grad = jnp.sum(gates * gate_grad, axis=1, keepdims=True)
    select_grad = gates * (gate_grad - mean_grad)
    logit_grad = jnp.sum(select_grad[:, :, None] * choose, axis=1)
    grad_normed_two = grad_normed_two + dot_nt(logit_grad, router_float, PRECISE)
    back_two, d_gain_ffn = norm_back(grad_normed_two, plain_two, scale_two, gain_two)
    grad_middle = grad_output + back_two
    own_grad_attn = grad_middle.astype(LOW)
    done1, block1 = early_weights(own_grad_attn)
    grad_blocks = [own_grad_attn]
    for bit in reversed(tensor_bits()):
        arrived = [tie(swap(block, "tensor", bit), done1) for block in grad_blocks]
        grad_blocks = grad_blocks + arrived if len(grad_blocks) == 1 else [
            *(grad_blocks[:1] + arrived[:1] + grad_blocks[1:] + arrived[1:])
        ]
    far_sums = [send_weights(0, None), send_weights(1, grad_blocks[2])]
    grad_attn = place_blocks(grad_blocks)
    sums, grad_one, fold = attend_back(
        qkv, mixed_heads, grad_attn, normed_low, w_qkv, w_out, lse, lines, ids_col, ids_row,
        heads, head_size, rows, [done1, far_sums[0]],
    )
    sums = tie(sums, far_sums[1])
    mixed = finish_mixed(fold)
    d_router = dot_tn(logit_grad, normed_two, PRECISE)
    done0, add_weights = finish_weights(block1, sums)
    sums = sum_expert(sums, done0)
    d_qkv = sums[: 3 * model_width].reshape(3, model_width, width)
    d_out = sums[3 * model_width :].T
    quarters = [
        lax.dynamic_slice_in_dim(grad_one, (mine ^ r) * own, own, 0) for r in range(tensor_size)
    ]
    held = quarters
    for bit in tensor_bits():
        keep = jnp.concatenate([held[r] for r in range(len(held)) if not r & 1], axis=0)
        give = jnp.concatenate([held[r] for r in range(len(held)) if r & 1], axis=0).astype(LOW)
        arrived = swap(give, "tensor", bit)
        held = keep.astype(WIDE) + arrived.astype(WIDE)
        held = [held[n * own : (n + 1) * own] for n in range(held.shape[0] // own)]
    grad_one = held[0]
    d_w_in, d_w_down = add_weights(far_sums)
    output_rows = place_blocks(gather_tensor((middle + mixed).astype(LOW)))
    plain_one, scale_one, _ = normalize(own_inputs, gain_one)
    back_one, d_gain_attn = norm_back(grad_one, plain_one, scale_one, gain_one)
    d_tokens = place_blocks(gather_tensor((grad_middle + back_one).astype(LOW)))

    d_bias = dot_nn_precise(fold, bucket_pick)
    d_bias = jnp.pad(d_bias, ((0, 0), (0, model_width - bucket_count)))
    here = (jnp.arange(tensor_size) == mine)[:, None, None]
    flat = jnp.concatenate(
        [
            d_gain_attn[None],
            d_gain_ffn[None],
            d_router,
            jnp.where(here, d_bias[None], 0.0).reshape(tensor_size * heads, model_width),
        ],
        axis=0,
    )
    flat = sum_small(flat)
    d_router = flat[2 : 2 + experts].T
    d_bias = lax.dynamic_slice_in_dim(flat, 2 + experts + mine * heads, heads, 0)
    return (
        output_rows,
        d_tokens,
        flat[0],
        flat[1],
        d_qkv,
        d_out,
        d_bias[:, :bucket_count].T,
        d_router,
        d_w_in,
        d_w_down,
    )


def solution(mesh):
    return jax.shard_map(
        body,
        mesh=mesh,
        in_specs=(
            P("expert", None),
            P("expert", None),
            P(),
            P(),
            P(None, None, "tensor"),
            P("tensor", None),
            P(None, "tensor"),
            P(),
            P("expert", None, "tensor"),
            P("expert", "tensor", None),
            P("expert", None),
            P("expert"),
            P(),
        ),
        out_specs=(
            P("expert", None),
            P("expert", None),
            P(),
            P(),
            P(None, None, "tensor"),
            P("tensor", None),
            P(None, "tensor"),
            P(),
            P("expert", None, "tensor"),
            P("expert", "tensor", None),
        ),
        check_vma=False,
    )
```

```python
import functools

import jax
import jax.numpy as jnp
from jax import lax
from jax.experimental import pallas as pl
from jax.experimental.pallas import tpu as pltpu
from jax.sharding import PartitionSpec as P

EPSILON = 1e-06
PRECISE = lax.Precision.HIGHEST
FLOOR_SCORE = -1e30
LOW = jnp.bfloat16
WIDE = jnp.float32
VMEM_BYTES = 62 * 1024 * 1024
QUERY_ROWS = 256


def dot_nn(left, right):
    return lax.dot_general(left, right, (((1,), (0,)), ((), ())), preferred_element_type=WIDE)


def dot_tn(left, right, precision=None):
    return lax.dot_general(
        left, right, (((0,), (0,)), ((), ())), precision=precision, preferred_element_type=WIDE
    )


def dot_nt(left, right, precision=None):
    return lax.dot_general(
        left, right, (((1,), (1,)), ((), ())), precision=precision, preferred_element_type=WIDE
    )


def dot_nn_precise(left, right):
    return jnp.dot(left, right, precision=PRECISE, preferred_element_type=WIDE)


def normalize(values, gain_vec):
    scale_rows = lax.rsqrt(jnp.mean(values * values, axis=-1, keepdims=True) + EPSILON)
    plain_rows = values * scale_rows
    return (plain_rows, scale_rows, plain_rows * gain_vec)


def norm_back(grad_in, plain_rows, scale_rows, gain_vec):
    gain_grad = jnp.sum(grad_in * plain_rows, axis=0)
    inner_grad = grad_in * gain_vec
    spread_grad = scale_rows * (
        inner_grad - plain_rows * jnp.mean(inner_grad * plain_rows, axis=-1, keepdims=True)
    )
    return (spread_grad, gain_grad)


def head_lanes(width, head_size, head):
    lane = lax.broadcasted_iota(jnp.int32, (1, width), 1)
    return ((lane >= head * head_size) & (lane < (head + 1) * head_size)).astype(LOW)


def build_strips(lines_ref, strip_ref, heads, rows, length):
    for head in range(heads):
        line = jnp.broadcast_to(lines_ref[head : head + 1, :], (rows, length + rows))
        strip_ref[head] = pltpu.roll(line, 0, 1, stride=1, stride_axis=0)[:, :length]


def strip_scores(query, key, strip_ref, head, first, rows, width, length, col_ids, row_ids):
    scores = dot_nt(query, key) + strip_ref[head, :, length - width :]
    return jnp.where(col_ids == row_ids, scores, FLOOR_SCORE)


def attend_kernel(heads, head_size, rows, qkv_ref, lines_ref, ids_col, ids_row, o_ref, lse_ref, strip_ref):
    length, width_all = qkv_ref.shape[1:]
    build_strips(lines_ref, strip_ref, heads, rows, length)
    scale = head_size ** (-0.5)
    for first in range(0, length, rows):
        width = first + rows
        query = qkv_ref[0, first:width, :]
        key = qkv_ref[1, :width, :]
        value = qkv_ref[2, :width, :]
        mixed = jnp.zeros((rows, width_all), WIDE)
        for head in range(heads):
            lanes = head_lanes(width_all, head_size, head)
            scores = strip_scores(
                query * (lanes * LOW(scale)), key, strip_ref, head, first, rows, width, length,
                ids_col[first:width, :], ids_row[:, :width],
            )
            row_max = jnp.max(scores, axis=-1, keepdims=True)
            exp_scores = jnp.exp(scores - row_max)
            row_total = jnp.sum(exp_scores, axis=-1, keepdims=True)
            probs = (exp_scores * (1.0 / row_total)).astype(LOW)
            mixed = mixed + dot_nn(probs, value) * lanes.astype(WIDE)
            lse_ref[first:width, head : head + 1] = row_max + jnp.log(row_total)
        o_ref[first:width, :] = mixed.astype(LOW)


def attend_back_kernel(
    heads, head_size, rows, tokens, qkv_ref, mixed_ref, grad_ref, normed_ref, w_qkv_ref, w_out_ref,
    lse_ref, lines_ref, ids_col, ids_row, *refs
):
    sums_ref, back_ref, fold_ref = refs[tokens : tokens + 3]
    strip_ref, grad_strip, do_ref, dqkv_ref, dk_acc, dv_acc = refs[tokens + 3 :]
    length, width_all = qkv_ref.shape[1:]
    build_strips(lines_ref, strip_ref, heads, rows, length)
    scale = head_size ** (-0.5)
    grad_strip[...] = jnp.zeros_like(grad_strip)
    dk_acc[...] = jnp.zeros_like(dk_acc)
    dv_acc[...] = jnp.zeros_like(dv_acc)
    do_ref[...] = dot_nt(grad_ref[...], w_out_ref[...]).astype(LOW)
    sums_ref[3 * width_all :] = dot_tn(mixed_ref[...], grad_ref[...]).astype(LOW)
    for first in range(0, length, rows):
        width = first + rows
        query = qkv_ref[0, first:width, :]
        key = qkv_ref[1, :width, :]
        value = qkv_ref[2, :width, :]
        grad_out = do_ref[first:width, :]
        dq = jnp.zeros((rows, width_all), WIDE)
        for head in range(heads):
            lanes = head_lanes(width_all, head_size, head)
            query_head = query * (lanes * LOW(scale))
            grad_head = grad_out * lanes
            scores = strip_scores(
                query_head, key, strip_ref, head, first, rows, width, length,
                ids_col[first:width, :], ids_row[:, :width],
            )
            probs = jnp.exp(scores - lse_ref[first:width, head : head + 1])
            grad_probs = dot_nt(grad_head, value)
            inner = jnp.sum(probs * grad_probs, axis=-1, keepdims=True)
            grad_scores = (probs * (grad_probs - inner)).astype(LOW)
            grad_strip[head, :, length - width :] += grad_scores.astype(WIDE)
            dv_acc[:width, :] += dot_tn(probs.astype(LOW), grad_head)
            dk_acc[:width, :] += dot_tn(grad_scores, query_head)
            dq = dq + dot_nn(grad_scores, key) * lanes.astype(WIDE)
        dqkv_ref[0, first:width, :] = (dq * scale).astype(LOW)
    dqkv_ref[1] = dk_acc[...].astype(LOW)
    dqkv_ref[2] = dv_acc[...].astype(LOW)
    for c in range(3):
        sums_ref[c * width_all : (c + 1) * width_all] = dot_tn(
            dqkv_ref[c], normed_ref[...]
        ).astype(LOW)
    for first in range(0, length, rows):
        part = slice(first, first + rows)
        back = dot_nt(dqkv_ref[0, part], w_qkv_ref[0])
        for c in (1, 2):
            back = back + dot_nt(dqkv_ref[c, part], w_qkv_ref[c])
        back_ref[part] = back.astype(LOW)
    line_width = length + rows
    for head in range(heads):
        folded = jnp.concatenate(
            [grad_strip[head], jnp.zeros((rows, rows), WIDE)], axis=1
        )
        left = rows
        while left > 1:
            left //= 2
            folded = folded[:left] + pltpu.roll(folded[left:], line_width - left, 1)
        fold_ref[head : head + 1, :] = folded


def attend(qkv, lines, ids_col, ids_row, heads, head_size, rows):
    _, length, width = qkv.shape
    return pl.pallas_call(
        functools.partial(attend_kernel, heads, head_size, rows),
        out_shape=(
            jax.ShapeDtypeStruct((length, width), LOW),
            jax.ShapeDtypeStruct((length, heads), WIDE),
        ),
        scratch_shapes=[pltpu.VMEM((heads, rows, length), WIDE)],
        compiler_params=pltpu.CompilerParams(vmem_limit_bytes=VMEM_BYTES),
        cost_estimate=pl.CostEstimate(
            flops=200 * length * length * width, bytes_accessed=1 << 22, transcendentals=0
        ),
        name="attend",
    )(qkv, lines, ids_col, ids_row)


def attend_back(
    qkv, mixed, grad_attn, normed, w_qkv, w_out, lse, lines, ids_col, ids_row,
    heads, head_size, rows, tokens,
):
    _, length, width = qkv.shape
    model_width = normed.shape[1]
    operands = (qkv, mixed, grad_attn, normed, w_qkv, w_out, lse, lines, ids_col, ids_row)
    return pl.pallas_call(
        functools.partial(attend_back_kernel, heads, head_size, rows, len(tokens)),
        in_specs=[pl.BlockSpec(memory_space=pltpu.VMEM)] * len(operands) + [ANYWHERE] * len(tokens),
        out_shape=(
            jax.ShapeDtypeStruct((4 * width, model_width), LOW),
            jax.ShapeDtypeStruct((length, model_width), LOW),
            jax.ShapeDtypeStruct((heads, length + rows), WIDE),
        ),
        scratch_shapes=[
            pltpu.VMEM((heads, rows, length), WIDE),
            pltpu.VMEM((heads, rows, length), WIDE),
            pltpu.VMEM((length, width), LOW),
            pltpu.VMEM((3, length, width), LOW),
            pltpu.VMEM((length, width), WIDE),
            pltpu.VMEM((length, width), WIDE),
        ],
        compiler_params=pltpu.CompilerParams(vmem_limit_bytes=VMEM_BYTES),
        cost_estimate=pl.CostEstimate(
            flops=200 * length * length * width, bytes_accessed=1 << 22, transcendentals=0
        ),
        name="attend_back",
    )(*operands, *tokens)


ANYWHERE = pl.BlockSpec(memory_space=pltpu.HBM)


def tie(values, *earlier):
    def kernel(*refs):
        pass

    return pl.pallas_call(
        kernel,
        out_shape=jax.ShapeDtypeStruct(values.shape, values.dtype),
        in_specs=[ANYWHERE] * (1 + len(earlier)),
        out_specs=ANYWHERE,
        input_output_aliases={0: 0},
        name="tie",
    )(values, *earlier)


def swap(values, axis_name, bit):
    size = lax.axis_size(axis_name)
    return lax.ppermute(values, axis_name, [(i, i ^ bit) for i in range(size)])


def tensor_bits():
    size = lax.axis_size("tensor")
    return [1 << b for b in range(size.bit_length() - 1)]


def gather_tensor(values):
    blocks = {0: values}
    for bit in reversed(tensor_bits()):
        blocks.update({r | bit: swap(block, "tensor", bit) for r, block in blocks.items()})
    return [blocks[r] for r in range(len(blocks))]


def place_blocks(blocks):
    rows = blocks[0].shape[0]
    count = len(blocks)

    def kernel(mine, *refs):
        for r in range(count):
            first = pl.multiple_of((mine[0] ^ r) * rows, rows)
            refs[count][pl.ds(first, rows)] = refs[r][...]

    return pl.pallas_call(
        kernel,
        out_shape=jax.ShapeDtypeStruct((count * rows,) + blocks[0].shape[1:], blocks[0].dtype),
        in_specs=[pl.BlockSpec(memory_space=pltpu.SMEM)]
        + [pl.BlockSpec(memory_space=pltpu.VMEM)] * count,
        out_specs=pl.BlockSpec(memory_space=pltpu.VMEM),
        name="place",
    )(lax.axis_index("tensor").astype(jnp.int32).reshape(1), *blocks)


def sum_small(values):
    for axis_name in ("tensor", "expert"):
        for b in range(lax.axis_size(axis_name).bit_length() - 1):
            values = values + swap(values, axis_name, 1 << b)
    return values


def sum_expert(values, beside):
    size = lax.axis_size("expert")
    parts = values.astype(LOW).reshape((size, values.shape[0] // size) + values.shape[1:])
    parts = tie(lax.all_to_all(parts, "expert", split_axis=0, concat_axis=0, tiled=True), beside)
    part = jnp.sum(parts.astype(WIDE), axis=0).astype(LOW)
    parts = jnp.broadcast_to(part[None], parts.shape)
    parts = lax.all_to_all(parts, "expert", split_axis=0, concat_axis=0, tiled=True)
    return parts.reshape(values.shape).astype(WIDE)


def pick_rows(near, far, chosen):
    rows = near.shape[0]
    return dot_nn(chosen[:, :rows], near) + dot_nn(chosen[:, rows:], far)


def gelu_pair(values):
    slope = (2.0 / jnp.pi) ** 0.5
    square = values * values
    bend = jnp.tanh(slope * values * (1.0 + 0.044715 * square))
    outer = 0.5 + 0.5 * bend
    steep = slope * (1.0 + 3 * 0.044715 * square)
    return values * outer, outer + 0.5 * values * (1.0 - bend * bend) * steep


def short_rows(rows):
    return rows * 9 // 16 // 16 * 16


def split_low(values, rounded=lambda values: values.astype(LOW).astype(WIDE)):
    pieces = []
    for _ in range(3):
        piece = rounded(values)
        pieces.append(piece.astype(LOW))
        values = values - piece
    return pieces


def round_low(values):
    return lax.reduce_precision(values, 8, 7)


def expert_kernel(blocks, chunk, experts, tokens, joined, meta, near, far, grads, *refs):
    weights, refs = refs[: 2 * blocks], refs[2 * blocks + tokens :]
    (kept_rows, kept_grads, count, hidden_out, pre_out), refs = refs[:5], refs[5:]
    if joined:
        backs, refs = refs[:2], refs[2:]
        mix_outs = None
    else:
        backs, mix_outs, refs = refs[:2], refs[2:4], refs[4:]
    weight_buf, grad_buf, hidden_buf, pre_buf, weight_sem, grad_sem, out_sem = refs
    span = grad_buf.shape[0]
    rows = span // 2
    model_width = near.shape[1]
    mine = meta[0]

    def weight_copy(n):
        return pltpu.make_async_copy(weights[n], weight_buf.at[n], weight_sem.at[n])

    def side_rows(side):
        return pl.ds(pl.multiple_of((mine ^ (2 * chunk + side)) * rows, rows), rows)

    def grad_copy(side):
        return pltpu.make_async_copy(
            grads.at[side_rows(side)], grad_buf.at[pl.ds(side * rows, rows)], grad_sem.at[side]
        )

    for side in (0, 1):
        grad_copy(side).start()
    for n in range(2 * blocks):
        weight_copy(n).start()

    def gates_of(payload):
        extra = payload[rows : rows + experts, :].astype(WIDE)
        here = lax.broadcasted_iota(jnp.int32, extra.shape, 0) == mine
        line = jnp.sum(jnp.where(here, extra, 0.0), axis=0, keepdims=True)
        return line[:, :rows] + line[:, rows : 2 * rows] + line[:, 2 * rows :]

    gate_row = jnp.concatenate([gates_of(near), gates_of(far)], axis=1)
    routed = gate_row != 0.0
    earlier = lax.broadcasted_iota(jnp.int32, (span, span), 0) < lax.broadcasted_iota(
        jnp.int32, (span, span), 1
    )
    routed_wide = routed.astype(WIDE)
    rank = dot_nn(
        jnp.broadcast_to(routed_wide, (8, span)).astype(LOW), earlier.astype(WIDE).astype(LOW)
    )[:1]
    rank = jnp.where(routed, rank, -1.0).astype(jnp.int32)
    total = jnp.sum(routed_wide).astype(jnp.int32)
    count[0] = total

    def run(taken):
        def out_copy(n, buffer, target, lane):
            return pltpu.make_async_copy(
                buffer.at[n, pl.ds(0, taken)], target.at[n, pl.ds(0, taken)], out_sem.at[lane, n]
            )

        chosen_wide = (rank == lax.broadcasted_iota(jnp.int32, (taken, span), 0)).astype(WIDE)
        chosen = chosen_wide.astype(LOW)
        picked = pick_rows(near[:rows], far[:rows], chosen).astype(LOW)
        gate_col = jnp.sum(chosen_wide * gate_row, axis=1, keepdims=True)
        for side in (0, 1):
            grad_copy(side).wait()
        grad_rows = pick_rows(grad_buf[:rows], grad_buf[rows:], chosen)
        gated = (gate_col * grad_rows).astype(LOW)
        kept_rows[:taken] = picked
        kept_grads[:taken] = gated
        expert_out = jnp.zeros((taken, model_width), WIDE)
        row_grad = jnp.zeros((taken, model_width), WIDE)
        for n in range(blocks):
            w_in, w_down = weight_buf.at[2 * n], weight_buf.at[2 * n + 1]
            weight_copy(2 * n).wait()
            weight_copy(2 * n + 1).wait()
            value, slope = gelu_pair(dot_nn(picked, w_in[...]))
            hidden = value.astype(LOW)
            hidden_buf[n, :taken] = hidden
            out_copy(n, hidden_buf, hidden_out, 0).start()
            pre_grad = (dot_nt(gated, w_down[...]) * slope).astype(LOW)
            pre_buf[n, :taken] = pre_grad
            out_copy(n, pre_buf, pre_out, 1).start()
            expert_out = expert_out + dot_nn(hidden, w_down[...]).astype(LOW).astype(WIDE)
            row_grad = row_grad + dot_nt(pre_grad, w_in[...]).astype(LOW).astype(WIDE)
        mixed = dot_tn(chosen, (gate_col * expert_out).astype(LOW)).astype(LOW)
        back = dot_tn(chosen, row_grad.astype(LOW)).astype(LOW)
        grad_col = jnp.sum(grad_rows * expert_out, axis=1, keepdims=True)
        gate_grad = jnp.sum(chosen_wide * grad_col, axis=0, keepdims=True)
        extra = payload_rows(rows, experts) - rows
        for side, back_out in enumerate(backs):
            part = slice(side * rows, (side + 1) * rows)
            back_out[:rows] = back[part]
            pieces = split_low(gate_grad[:, part])
            line = jnp.concatenate([piece.astype(WIDE) for piece in pieces], axis=1)
            here = lax.broadcasted_iota(jnp.int32, (extra, model_width), 0) == mine
            back_out[rows : rows + extra] = jnp.where(here, line, 0.0).astype(LOW)
            if joined:
                back_out[rows + extra :] = mixed[part]
            else:
                mix_outs[side][...] = mixed[part]
        for n in range(blocks):
            out_copy(n, hidden_buf, hidden_out, 0).wait()
            out_copy(n, pre_buf, pre_out, 1).wait()

    few = total <= short_rows(span)

    @pl.when(few)
    def _():
        run(short_rows(span))

    @pl.when(jnp.logical_not(few))
    def _():
        run(span)


def payload_rows(rows, experts):
    return rows + -(-experts // 16) * 16


def expert_chunk(chunk, experts, rows, joined, meta, near, far, grads, weights, tokens):
    payload, model_width = near.shape
    span = 2 * rows
    blocks = len(weights) // 2
    block_width = weights[0].shape[1]
    low = functools.partial(jax.ShapeDtypeStruct, dtype=LOW)
    vmem = pl.BlockSpec(memory_space=pltpu.VMEM)
    smem = pl.BlockSpec(memory_space=pltpu.SMEM)
    sides = [low((payload + rows, model_width))] * 2
    if not joined:
        sides = [low((payload, model_width))] * 2 + [low((rows, model_width))] * 2
    return pl.pallas_call(
        functools.partial(expert_kernel, blocks, chunk, experts, len(tokens), joined),
        out_shape=(
            low((span, model_width)),
            low((span, model_width)),
            jax.ShapeDtypeStruct((1,), jnp.int32),
            low((blocks, span, block_width)),
            low((blocks, span, block_width)),
            *sides,
        ),
        in_specs=[smem, vmem, vmem] + [ANYWHERE] * (1 + len(weights) + len(tokens)),
        out_specs=(vmem, vmem, smem, ANYWHERE, ANYWHERE) + (vmem,) * len(sides),
        scratch_shapes=[
            pltpu.VMEM((2 * blocks,) + weights[0].shape, LOW),
            pltpu.VMEM((span, model_width), LOW),
            pltpu.VMEM((blocks, span, block_width), LOW),
            pltpu.VMEM((blocks, span, block_width), LOW),
            pltpu.SemaphoreType.DMA((2 * blocks,)),
            pltpu.SemaphoreType.DMA((2,)),
            pltpu.SemaphoreType.DMA((2, blocks)),
        ],
        compiler_params=pltpu.CompilerParams(vmem_limit_bytes=VMEM_BYTES),
        cost_estimate=pl.CostEstimate(
            flops=200 * short_rows(span) * model_width * block_width * blocks,
            bytes_accessed=1 << 24,
            transcendentals=0,
        ),
        name="expert_chunk",
    )(meta, near, far, grads, *weights, *tokens)


def weight_grad_kernel(chunks, block, tokens, *refs):
    counts, refs = refs[:chunks], refs[chunks:]
    kept, refs = refs[: 4 * chunks], refs[4 * chunks + tokens :]
    done, refs = refs[0], refs[1:]
    done[0] = counts[0][0]
    if block:
        out_ref, refs = refs[0], refs[1:]
    in_grad, down_grad, row_buf, grad_buf, hidden_buf, pre_buf, sem = refs
    span = row_buf.shape[1]

    def by_count(chunk, action):
        few = counts[chunk][0] <= short_rows(span)

        @pl.when(few)
        def _():
            action(short_rows(span))

        @pl.when(jnp.logical_not(few))
        def _():
            action(span)

    def copies(chunk, taken):
        rows, grads, hidden, pre = kept[4 * chunk : 4 * chunk + 4]
        part = pl.ds(0, taken)
        return [
            pltpu.make_async_copy(source, target, sem.at[chunk, n])
            for n, (source, target) in enumerate(
                (
                    (rows.at[part], row_buf.at[chunk, part]),
                    (grads.at[part], grad_buf.at[chunk, part]),
                    (hidden.at[block, part], hidden_buf.at[chunk, part]),
                    (pre.at[block, part], pre_buf.at[chunk, part]),
                )
            )
        ]

    for chunk in range(chunks):
        by_count(chunk, lambda taken, chunk=chunk: [copy.start() for copy in copies(chunk, taken)])

    def add(chunk, taken):
        for copy in copies(chunk, taken):
            copy.wait()
        in_part = dot_tn(row_buf[chunk, :taken], pre_buf[chunk, :taken])
        down_part = dot_tn(hidden_buf[chunk, :taken], grad_buf[chunk, :taken])
        if chunk == 0:
            in_grad[...] = in_part
            down_grad[...] = down_part
        elif chunk == chunks - 1 and block:
            out_ref[0] = (in_grad[...] + in_part).astype(LOW)
            out_ref[1] = (down_grad[...] + down_part).astype(LOW)
        else:
            in_grad[...] += in_part
            down_grad[...] += down_part

    for chunk in range(chunks):
        by_count(chunk, functools.partial(add, chunk))


def weight_grads(block, counts, kept, tokens):
    chunks = len(kept)
    span, model_width = kept[0][0].shape
    block_width = kept[0][2].shape[2]
    accumulators = [(model_width, block_width), (block_width, model_width)]
    if block:
        out_shape = (jax.ShapeDtypeStruct((2, model_width, block_width), LOW),)
        extra = [pltpu.VMEM(shape, WIDE) for shape in accumulators]
    else:
        out_shape = tuple(jax.ShapeDtypeStruct(shape, WIDE) for shape in accumulators)
        extra = []
    return pl.pallas_call(
        functools.partial(weight_grad_kernel, chunks, block, len(tokens)),
        out_shape=(jax.ShapeDtypeStruct((1,), jnp.int32),) + out_shape,
        out_specs=(pl.BlockSpec(memory_space=pltpu.SMEM),)
        + (pl.BlockSpec(memory_space=pltpu.VMEM),) * len(out_shape),
        in_specs=[pl.BlockSpec(memory_space=pltpu.SMEM)] * chunks
        + [ANYWHERE] * (4 * chunks + len(tokens)),
        scratch_shapes=extra
        + [
            pltpu.VMEM((chunks, span, model_width), LOW),
            pltpu.VMEM((chunks, span, model_width), LOW),
            pltpu.VMEM((chunks, span, block_width), LOW),
            pltpu.VMEM((chunks, span, block_width), LOW),
            pltpu.SemaphoreType.DMA((chunks, 4)),
        ],
        compiler_params=pltpu.CompilerParams(vmem_limit_bytes=VMEM_BYTES),
        cost_estimate=pl.CostEstimate(
            flops=120 * chunks * short_rows(span) * model_width * block_width,
            bytes_accessed=1 << 23,
            transcendentals=0,
        ),
        name="weight_grads",
    )(*counts, *[array for four in kept for array in four], *tokens)


def dense_experts(normed_low, grad_low, gates, choose, routes, gathered):
    rows, model_width = normed_low.shape
    experts = choose.shape[2]
    size = lax.axis_size("expert")
    chunks = size // 2
    meta = lax.axis_index("expert").astype(jnp.int32).reshape(1)
    w_in_blocks, w_down_own, w_down_far, grad_all = gathered
    dense_gates = jnp.sum(gates[:, :, None] * choose, axis=1).T
    gate_rows = jnp.concatenate(split_low(dense_gates, round_low), axis=1)
    payload = jnp.concatenate([normed_low, gate_rows], axis=0)
    payload = jnp.pad(payload, ((0, payload_rows(rows, experts) - payload.shape[0]), (0, 0)))
    run = functools.partial(expert_chunk, rows=rows, experts=experts, meta=meta, grads=grad_all)

    def side_swap(values):
        return swap(values, "expert", 1)

    def plane_swap(chunk, values):
        return swap(values, "expert", 2 * chunk)

    far = [side_swap(payload)]
    near = [payload, plane_swap(1, payload)]
    near[1] = tie(near[1], far[0])
    far.append(side_swap(near[1]))
    near.append(plane_swap(2, tie(payload, near[1])))
    last_down = tie(w_down_far, near[1])
    in_blocks = w_in_blocks
    down_blocks = [w_down_own, swap(w_down_own, "tensor", 1), last_down, swap(last_down, "tensor", 1)]
    weights = [block for pair in zip(in_blocks, down_blocks) for block in pair]

    kept, counts, held, flown, mixes, backs = [], [], [], [], [], []

    def chunk_step(chunk, tokens):
        joined = chunk < 2
        rows_c, grads_c, count, hidden, pre, back_near, back_far, *mixed = run(
            chunk, joined=joined, near=near[chunk], far=far[chunk], weights=weights, tokens=tokens
        )
        kept.append((rows_c, grads_c, hidden, pre))
        counts.append(count)
        mixes.append(mixed)
        backs.append((back_near, side_swap(back_far)))

    def hold(chunk, token):
        back_near, arrived = backs[chunk]
        return (back_near.astype(WIDE) + tie(arrived, token).astype(WIDE)).astype(LOW)

    chunk_step(0, [])
    near[2] = tie(near[2], counts[0])
    far.append(side_swap(near[2]))
    near.append(plane_swap(3, tie(payload, near[2])))
    chunk_step(1, [counts[0]])
    near[3] = tie(near[3], counts[1])
    far.append(side_swap(near[3]))
    held.append(hold(0, counts[1]))
    chunk_step(2, [counts[1], held[0]])
    held.append(hold(1, counts[2]))
    flown.append(plane_swap(1, held[1]))
    chunk_step(3, [counts[2], held[1]])
    held.append(hold(2, counts[3]))
    flown[0] = tie(flown[0], counts[3])
    flown.append(plane_swap(2, held[2]))
    joint = held[0].astype(WIDE) + flown[0].astype(WIDE)
    grads_of = functools.partial(weight_grads, counts=counts, kept=kept)
    done3, block3 = grads_of(3, tokens=[flown[0], held[2]])
    held.append(hold(3, done3))
    flown.append(plane_swap(3, held[3]))
    core3 = swap(block3, "tensor", 1)
    late = [side_swap(tie(mixes[chunk][1], held[3])) for chunk in (2, 3)]
    done2, block2 = grads_of(2, tokens=[done3, held[3]])
    flown[1] = tie(flown[1], done2)
    flown[2] = tie(flown[2], done2)
    chip_sum = (block2.astype(WIDE) + tie(core3, done2).astype(WIDE)).astype(LOW)
    late = [
        (mixes[chunk][0].astype(WIDE) + tie(arrived, done2).astype(WIDE)).astype(LOW)
        for chunk, arrived in zip((2, 3), late)
    ]
    late = [plane_swap(chunk, values) for chunk, values in zip((2, 3), late)]
    payload = payload.shape[0]
    row_grad = joint[:payload] + flown[1].astype(WIDE) + flown[2].astype(WIDE)
    tail = row_grad[rows : rows + experts]
    gate_grad = tail[:, :rows] + tail[:, rows : 2 * rows] + tail[:, 2 * rows :]
    gate_grad = jnp.sum(gate_grad.T[:, None, :] * choose, axis=-1)

    def early_weights(token):
        return grads_of(1, tokens=[token])

    def send_weights(n, arrived):
        sent = chip_sum[n] if arrived is None else tie(chip_sum[n], arrived)
        return swap(sent, "tensor", 2)

    def finish_mixed(token):
        mixed = joint[payload:]
        for values in late:
            mixed = mixed + tie(values, token).astype(WIDE)
        return mixed

    def finish_weights(block1, token):
        done0, *block0 = grads_of(0, tokens=[token])
        near_sum = tie(swap(block1, "tensor", 1), token)
        return done0, lambda far_sums: tuple(
            (block0[n] + near_sum[n].astype(WIDE) + far_sums[n].astype(WIDE))[None] for n in (0, 1)
        )

    return gate_grad, row_grad[:rows], early_weights, send_weights, finish_mixed, finish_weights


def pick_slots(buffer, flat_experts, slot_index, first_slot, slot_count):
    local_slot = slot_index - first_slot
    inside = ((local_slot >= 0) & (local_slot < slot_count)).astype(WIDE)
    rows = buffer[flat_experts, 0, jnp.clip(local_slot, 0, slot_count - 1)].astype(WIDE)
    return rows * inside[:, None]


def slot_experts(normed_low, grad_low, gates, choose, routes, gathered):
    w_in, w_down = gathered
    own = normed_low.shape[0]
    tensor_size = lax.axis_size("tensor")
    sources = lax.axis_size("expert")
    first_own = lax.axis_index("tensor") * own
    length = own * tensor_size
    experts = choose.shape[2]
    model_width = normed_low.shape[1]
    capacity = 4 * length // experts
    share_rows = capacity // tensor_size
    first_share = lax.axis_index("tensor") * share_rows
    normed_all = lax.all_gather(normed_low, "tensor", axis=0, tiled=True)
    grad_all = lax.all_gather(grad_low, "tensor", axis=0, tiled=True)
    gates_all = lax.all_gather(gates, "tensor", axis=0, tiled=True)
    flat_experts = routes.reshape(-1)
    marks = (flat_experts[:, None] == jnp.arange(experts)[None, :]).astype(jnp.int32)
    slot_index = jnp.sum((jnp.cumsum(marks, axis=0) - 1) * marks, axis=1)
    token_index = jnp.arange(2 * length) // 2

    def send(values):
        empty = jnp.zeros((experts, 1, capacity, model_width), LOW)
        placed = empty.at[flat_experts, 0, slot_index].set(values)
        arrived = lax.all_to_all(placed, "expert", split_axis=0, concat_axis=1, tiled=True)
        return arrived.reshape(sources * capacity, model_width)

    def give_back(values):
        summed = lax.psum_scatter(
            values.reshape(sources, capacity, model_width), "tensor", scatter_dimension=1, tiled=True
        )
        returned = lax.all_to_all(
            summed.reshape(1, sources, share_rows, model_width),
            "expert", split_axis=1, concat_axis=0, tiled=True,
        )
        return pick_slots(returned, flat_experts, slot_index, first_share, share_rows).reshape(
            length, 2, model_width
        )

    expert_rows = send(normed_all[token_index])
    grad_wide = grad_all.astype(WIDE)
    toward = (gates_all[:, :, None] * grad_wide[:, None, :]).astype(LOW)
    grad_rows = send(toward.reshape(2 * length, model_width))
    hidden_pre = dot_nn(expert_rows, w_in[0])
    hidden, gelu_back = jax.vjp(functools.partial(jax.nn.gelu, approximate=True), hidden_pre)
    hidden = hidden.astype(LOW)
    picked = give_back(dot_nn(hidden, w_down[0]).astype(LOW))
    grad_pre = gelu_back(dot_nt(grad_rows, w_down[0]))[0].astype(LOW)
    d_w_down = dot_tn(hidden, grad_rows)[None]
    d_w_in = dot_tn(expert_rows, grad_pre)[None]
    back_rows = give_back(dot_nt(grad_pre, w_in[0]).astype(LOW))
    mixed = jnp.sum(gates_all[:, :, None] * picked, axis=1)
    gate_grad = jnp.sum(picked * grad_wide[:, None, :], axis=-1)
    mixed, gate_grad, row_grad = (
        lax.dynamic_slice_in_dim(values, first_own, own, 0)
        for values in lax.psum((mixed, gate_grad, jnp.sum(back_rows, axis=1)), "tensor")
    )
    token = gate_grad[:1, :1]
    return (
        gate_grad,
        row_grad,
        lambda token: (token, token),
        lambda n, arrived: token,
        lambda token: mixed,
        lambda block1, token: (token, lambda far_sums: (d_w_in, d_w_down)),
    )


def body(
    tokens,
    cotangent,
    gain_attn,
    gain_ffn,
    w_qkv,
    w_out,
    bias_table,
    router,
    w_in,
    w_down,
    routes,
    sequence_ids,
    rel_buckets,
):
    length, model_width = tokens.shape
    rows = min(QUERY_ROWS, length)
    bucket_count, heads = bias_table.shape
    width = w_qkv.shape[2]
    head_size = width // heads
    experts = router.shape[1]
    tensor_size = lax.axis_size("tensor")
    own = length // tensor_size
    mine = lax.axis_index("tensor")

    def own_rows(values):
        return lax.dynamic_slice_in_dim(values, mine * own, own, 0)

    gain_one = gain_attn.astype(WIDE)
    gain_two = gain_ffn.astype(WIDE)
    grad_low = own_rows(cotangent)
    grad_output = grad_low.astype(WIDE)
    own_inputs = own_rows(tokens).astype(WIDE)
    own_routes = own_rows(routes)
    out_blocks = gather_tensor(w_out)

    _, _, normed_one = normalize(tokens.astype(WIDE), gain_one)
    normed_low = normed_one.astype(LOW)
    qkv = jnp.einsum("td,cdh->cth", normed_low, w_qkv, preferred_element_type=WIDE).astype(LOW)
    line_width = length + rows
    place = jnp.arange(line_width)
    distance = jnp.where(place < length, length - rows - place, 2 * length - place)
    buckets = jnp.concatenate(
        [
            rel_buckets[: length - rows + 1][::-1],
            jnp.zeros((rows,), jnp.int32),
            rel_buckets[length - rows + 1 :][::-1],
        ]
    )
    bucket_pick = (
        (buckets[:, None] == jnp.arange(bucket_count)[None, :]) & (distance >= 0)[:, None]
    ).astype(WIDE)
    lines = dot_tn(bias_table.astype(WIDE), bucket_pick.T, PRECISE)
    lines = jnp.where((distance >= 0)[None, :], lines, FLOOR_SCORE)
    ids_col = sequence_ids[:, None]
    ids_row = sequence_ids[None, :]
    mixed_heads, lse = attend(qkv, lines, ids_col, ids_row, heads, head_size, rows)

    whole_width = (
        lax.axis_size("expert") == 8
        and tensor_size == 4
        and 3 * own == model_width
        and w_in.shape[2] == model_width
    )
    if whole_width:
        w_in_far = tie(swap(w_in[0], "tensor", 2), lse)
        w_in_near = swap(w_in[0], "tensor", 1)

    half = [mixed_heads]
    tags = [0]
    span = length
    for bit in reversed(tensor_bits()):
        span //= 2
        keep_at = jnp.where((mine & bit) != 0, span, 0)
        give_at = span - keep_at
        given = [lax.dynamic_slice_in_dim(block, give_at, span, 0) for block in half]
        if whole_width and len(half) == 1:
            given = [tie(given[0], w_in_far)]
        arrived = [swap(block, "tensor", bit) for block in given]
        half = [lax.dynamic_slice_in_dim(block, keep_at, span, 0) for block in half] + arrived
        tags = tags + [tag | bit for tag in tags]
    attention = sum(dot_nn(block, out_blocks[tag]) for tag, block in zip(tags, half))
    middle = own_inputs + attention
    plain_two, scale_two, normed_two = normalize(middle, gain_two)
    router_float = router.astype(WIDE)
    logits = jnp.dot(normed_two, router_float, precision=PRECISE)
    choose = (own_routes[:, :, None] == jnp.arange(experts)[None, None, :]).astype(WIDE)
    chosen = jnp.sum(logits[:, None, :] * choose, axis=-1)
    gates = jax.nn.softmax(chosen, axis=1)

    if whole_width:
        w_down_own = tie(w_down[0], half[1])
        gathered = (
            [w_in[0], w_in_near, w_in_far, swap(w_in_far, "tensor", 1)],
            w_down_own,
            swap(w_down_own, "tensor", 2),
            lax.all_gather(grad_low, "expert", axis=0, tiled=True),
        )
    else:
        gathered = (w_in, w_down)
    run_experts = dense_experts if whole_width else slot_experts
    gate_grad, grad_normed_two, early_weights, send_weights, finish_mixed, finish_weights = run_experts(
        normed_two.astype(LOW), grad_low, gates, choose, routes, gathered
    )

    mean_grad = jnp.sum(gates * gate_grad, axis=1, keepdims=True)
    select_grad = gates * (gate_grad - mean_grad)
    logit_grad = jnp.sum(select_grad[:, :, None] * choose, axis=1)
    grad_normed_two = grad_normed_two + dot_nt(logit_grad, router_float, PRECISE)
    back_two, d_gain_ffn = norm_back(grad_normed_two, plain_two, scale_two, gain_two)
    grad_middle = grad_output + back_two
    own_grad_attn = grad_middle.astype(LOW)
    done1, block1 = early_weights(own_grad_attn)
    grad_blocks = [own_grad_attn]
    for bit in reversed(tensor_bits()):
        arrived = [tie(swap(block, "tensor", bit), done1) for block in grad_blocks]
        grad_blocks = grad_blocks + arrived if len(grad_blocks) == 1 else [
            *(grad_blocks[:1] + arrived[:1] + grad_blocks[1:] + arrived[1:])
        ]
    far_sums = [send_weights(0, None), send_weights(1, grad_blocks[2])]
    grad_attn = place_blocks(grad_blocks)
    sums, grad_one, fold = attend_back(
        qkv, mixed_heads, grad_attn, normed_low, w_qkv, w_out, lse, lines, ids_col, ids_row,
        heads, head_size, rows, [done1, far_sums[0]],
    )
    sums = tie(sums, far_sums[1])
    mixed = finish_mixed(fold)
    d_router = dot_tn(logit_grad, normed_two, PRECISE)
    done0, add_weights = finish_weights(block1, sums)
    sums = sum_expert(sums, done0)
    d_qkv = sums[: 3 * width].reshape(3, width, model_width).transpose(0, 2, 1)
    d_out = sums[3 * width :]
    quarters = [
        lax.dynamic_slice_in_dim(grad_one, (mine ^ r) * own, own, 0) for r in range(tensor_size)
    ]
    held = quarters
    for bit in tensor_bits():
        keep = jnp.concatenate([held[r] for r in range(len(held)) if not r & 1], axis=0)
        give = jnp.concatenate([held[r] for r in range(len(held)) if r & 1], axis=0).astype(LOW)
        arrived = swap(give, "tensor", bit)
        held = keep.astype(WIDE) + arrived.astype(WIDE)
        held = [held[n * own : (n + 1) * own] for n in range(held.shape[0] // own)]
    grad_one = held[0]
    d_w_in, d_w_down = add_weights(far_sums)
    output_rows = place_blocks(gather_tensor((middle + mixed).astype(LOW)))
    plain_one, scale_one, _ = normalize(own_inputs, gain_one)
    back_one, d_gain_attn = norm_back(grad_one, plain_one, scale_one, gain_one)
    d_tokens = place_blocks(gather_tensor((grad_middle + back_one).astype(LOW)))

    d_bias = dot_nn_precise(fold, bucket_pick)
    d_bias = jnp.pad(d_bias, ((0, 0), (0, model_width - bucket_count)))
    here = (jnp.arange(tensor_size) == mine)[:, None, None]
    flat = jnp.concatenate(
        [
            d_gain_attn[None],
            d_gain_ffn[None],
            d_router,
            jnp.where(here, d_bias[None], 0.0).reshape(tensor_size * heads, model_width),
        ],
        axis=0,
    )
    flat = sum_small(flat)
    d_router = flat[2 : 2 + experts].T
    d_bias = lax.dynamic_slice_in_dim(flat, 2 + experts + mine * heads, heads, 0)
    return (
        output_rows,
        d_tokens,
        flat[0],
        flat[1],
        d_qkv,
        d_out,
        d_bias[:, :bucket_count].T,
        d_router,
        d_w_in,
        d_w_down,
    )


def solution(mesh):
    return jax.shard_map(
        body,
        mesh=mesh,
        in_specs=(
            P("expert", None),
            P("expert", None),
            P(),
            P(),
            P(None, None, "tensor"),
            P("tensor", None),
            P(None, "tensor"),
            P(),
            P("expert", None, "tensor"),
            P("expert", "tensor", None),
            P("expert", None),
            P("expert"),
            P(),
        ),
        out_specs=(
            P("expert", None),
            P("expert", None),
            P(),
            P(),
            P(None, None, "tensor"),
            P("tensor", None),
            P(None, "tensor"),
            P(),
            P("expert", None, "tensor"),
            P("expert", "tensor", None),
        ),
        check_vma=False,
    )
```

```python
import functools

import jax
import jax.numpy as jnp
from jax import lax
from jax.experimental import pallas as pl
from jax.experimental.pallas import tpu as pltpu
from jax.sharding import PartitionSpec as P

EPSILON = 1e-06
PRECISE = lax.Precision.HIGHEST
FLOOR_SCORE = -1e30
LOW = jnp.bfloat16
WIDE = jnp.float32
VMEM_BYTES = 62 * 1024 * 1024
QUERY_ROWS = 256


def dot_nn(left, right):
    return lax.dot_general(left, right, (((1,), (0,)), ((), ())), preferred_element_type=WIDE)


def dot_tn(left, right, precision=None):
    return lax.dot_general(
        left, right, (((0,), (0,)), ((), ())), precision=precision, preferred_element_type=WIDE
    )


def dot_nt(left, right, precision=None):
    return lax.dot_general(
        left, right, (((1,), (1,)), ((), ())), precision=precision, preferred_element_type=WIDE
    )


def dot_nn_precise(left, right):
    return jnp.dot(left, right, precision=PRECISE, preferred_element_type=WIDE)


def normalize(values, gain_vec):
    scale_rows = lax.rsqrt(jnp.mean(values * values, axis=-1, keepdims=True) + EPSILON)
    plain_rows = values * scale_rows
    return (plain_rows, scale_rows, plain_rows * gain_vec)


def norm_back(grad_in, plain_rows, scale_rows, gain_vec):
    gain_grad = jnp.sum(grad_in * plain_rows, axis=0)
    inner_grad = grad_in * gain_vec
    spread_grad = scale_rows * (
        inner_grad - plain_rows * jnp.mean(inner_grad * plain_rows, axis=-1, keepdims=True)
    )
    return (spread_grad, gain_grad)


def head_lanes(width, head_size, head):
    lane = lax.broadcasted_iota(jnp.int32, (1, width), 1)
    return ((lane >= head * head_size) & (lane < (head + 1) * head_size)).astype(LOW)


def build_strips(lines_ref, strip_ref, heads, rows, length):
    for head in range(heads):
        line = jnp.broadcast_to(lines_ref[head : head + 1, :], (rows, length + rows))
        strip_ref[head] = pltpu.roll(line, 0, 1, stride=1, stride_axis=0)[:, :length]


def strip_scores(query, key, strip_ref, head, first, rows, width, length, col_ids, row_ids):
    scores = dot_nt(query, key) + strip_ref[head, :, length - width :]
    return jnp.where(col_ids == row_ids, scores, FLOOR_SCORE)


def attend_kernel(heads, head_size, rows, qkv_ref, lines_ref, ids_col, ids_row, o_ref, lse_ref, strip_ref):
    length, width_all = qkv_ref.shape[1:]
    build_strips(lines_ref, strip_ref, heads, rows, length)
    scale = head_size ** (-0.5)
    for first in range(0, length, rows):
        width = first + rows
        query = qkv_ref[0, first:width, :]
        key = qkv_ref[1, :width, :]
        value = qkv_ref[2, :width, :]
        mixed = jnp.zeros((rows, width_all), WIDE)
        for head in range(heads):
            lanes = head_lanes(width_all, head_size, head)
            scores = strip_scores(
                query * (lanes * LOW(scale)), key, strip_ref, head, first, rows, width, length,
                ids_col[first:width, :], ids_row[:, :width],
            )
            row_max = jnp.max(scores, axis=-1, keepdims=True)
            exp_scores = jnp.exp(scores - row_max)
            row_total = jnp.sum(exp_scores, axis=-1, keepdims=True)
            probs = (exp_scores * (1.0 / row_total)).astype(LOW)
            mixed = mixed + dot_nn(probs, value) * lanes.astype(WIDE)
            lse_ref[first:width, head : head + 1] = row_max + jnp.log(row_total)
        o_ref[first:width, :] = mixed.astype(LOW)


def attend_back_kernel(
    heads, head_size, rows, tokens, qkv_ref, mixed_ref, grad_ref, normed_ref, w_qkv_ref, w_out_ref,
    lse_ref, lines_ref, ids_col, ids_row, *refs
):
    sums_ref, back_ref, fold_ref = refs[tokens : tokens + 3]
    strip_ref, grad_strip, do_ref, dqkv_ref, dk_acc, dv_acc = refs[tokens + 3 :]
    length, width_all = qkv_ref.shape[1:]
    build_strips(lines_ref, strip_ref, heads, rows, length)
    scale = head_size ** (-0.5)
    grad_strip[...] = jnp.zeros_like(grad_strip)
    dk_acc[...] = jnp.zeros_like(dk_acc)
    dv_acc[...] = jnp.zeros_like(dv_acc)
    do_ref[...] = dot_nt(grad_ref[...], w_out_ref[...]).astype(LOW)
    sums_ref[3 * width_all :] = dot_tn(mixed_ref[...], grad_ref[...]).astype(LOW)
    for first in range(0, length, rows):
        width = first + rows
        query = qkv_ref[0, first:width, :]
        key = qkv_ref[1, :width, :]
        value = qkv_ref[2, :width, :]
        grad_out = do_ref[first:width, :]
        dq = jnp.zeros((rows, width_all), WIDE)
        for head in range(heads):
            lanes = head_lanes(width_all, head_size, head)
            query_head = query * (lanes * LOW(scale))
            grad_head = grad_out * lanes
            scores = strip_scores(
                query_head, key, strip_ref, head, first, rows, width, length,
                ids_col[first:width, :], ids_row[:, :width],
            )
            probs = jnp.exp(scores - lse_ref[first:width, head : head + 1])
            grad_probs = dot_nt(grad_head, value)
            inner = jnp.sum(probs * grad_probs, axis=-1, keepdims=True)
            grad_scores = (probs * (grad_probs - inner)).astype(LOW)
            grad_strip[head, :, length - width :] += grad_scores.astype(WIDE)
            dv_acc[:width, :] += dot_tn(probs.astype(LOW), grad_head)
            dk_acc[:width, :] += dot_tn(grad_scores, query_head)
            dq = dq + dot_nn(grad_scores, key) * lanes.astype(WIDE)
        dqkv_ref[0, first:width, :] = (dq * scale).astype(LOW)
    dqkv_ref[1] = dk_acc[...].astype(LOW)
    dqkv_ref[2] = dv_acc[...].astype(LOW)
    for c in range(3):
        sums_ref[c * width_all : (c + 1) * width_all] = dot_tn(
            dqkv_ref[c], normed_ref[...]
        ).astype(LOW)
    for first in range(0, length, rows):
        part = slice(first, first + rows)
        back = dot_nt(dqkv_ref[0, part], w_qkv_ref[0])
        for c in (1, 2):
            back = back + dot_nt(dqkv_ref[c, part], w_qkv_ref[c])
        back_ref[part] = back.astype(LOW)
    line_width = length + rows
    for head in range(heads):
        folded = jnp.concatenate(
            [grad_strip[head], jnp.zeros((rows, rows), WIDE)], axis=1
        )
        left = rows
        while left > 1:
            left //= 2
            folded = folded[:left] + pltpu.roll(folded[left:], line_width - left, 1)
        fold_ref[head : head + 1, :] = folded


def attend(qkv, lines, ids_col, ids_row, heads, head_size, rows):
    _, length, width = qkv.shape
    return pl.pallas_call(
        functools.partial(attend_kernel, heads, head_size, rows),
        out_shape=(
            jax.ShapeDtypeStruct((length, width), LOW),
            jax.ShapeDtypeStruct((length, heads), WIDE),
        ),
        scratch_shapes=[pltpu.VMEM((heads, rows, length), WIDE)],
        compiler_params=pltpu.CompilerParams(vmem_limit_bytes=VMEM_BYTES),
        cost_estimate=pl.CostEstimate(
            flops=200 * length * length * width, bytes_accessed=1 << 22, transcendentals=0
        ),
        name="attend",
    )(qkv, lines, ids_col, ids_row)


def attend_back(
    qkv, mixed, grad_attn, normed, w_qkv, w_out, lse, lines, ids_col, ids_row,
    heads, head_size, rows, tokens,
):
    _, length, width = qkv.shape
    model_width = normed.shape[1]
    operands = (qkv, mixed, grad_attn, normed, w_qkv, w_out, lse, lines, ids_col, ids_row)
    return pl.pallas_call(
        functools.partial(attend_back_kernel, heads, head_size, rows, len(tokens)),
        in_specs=[pl.BlockSpec(memory_space=pltpu.VMEM)] * len(operands) + [ANYWHERE] * len(tokens),
        out_shape=(
            jax.ShapeDtypeStruct((4 * width, model_width), LOW),
            jax.ShapeDtypeStruct((length, model_width), LOW),
            jax.ShapeDtypeStruct((heads, length + rows), WIDE),
        ),
        scratch_shapes=[
            pltpu.VMEM((heads, rows, length), WIDE),
            pltpu.VMEM((heads, rows, length), WIDE),
            pltpu.VMEM((length, width), LOW),
            pltpu.VMEM((3, length, width), LOW),
            pltpu.VMEM((length, width), WIDE),
            pltpu.VMEM((length, width), WIDE),
        ],
        compiler_params=pltpu.CompilerParams(vmem_limit_bytes=VMEM_BYTES),
        cost_estimate=pl.CostEstimate(
            flops=200 * length * length * width, bytes_accessed=1 << 22, transcendentals=0
        ),
        name="attend_back",
    )(*operands, *tokens)


ANYWHERE = pl.BlockSpec(memory_space=pltpu.HBM)


def tie(values, *earlier):
    def kernel(*refs):
        pass

    return pl.pallas_call(
        kernel,
        out_shape=jax.ShapeDtypeStruct(values.shape, values.dtype),
        in_specs=[ANYWHERE] * (1 + len(earlier)),
        out_specs=ANYWHERE,
        input_output_aliases={0: 0},
        name="tie",
    )(values, *earlier)


def swap(values, axis_name, bit):
    size = lax.axis_size(axis_name)
    return lax.ppermute(values, axis_name, [(i, i ^ bit) for i in range(size)])


def tensor_bits():
    size = lax.axis_size("tensor")
    return [1 << b for b in range(size.bit_length() - 1)]


def gather_tensor(values):
    blocks = {0: values}
    for bit in reversed(tensor_bits()):
        blocks.update({r | bit: swap(block, "tensor", bit) for r, block in blocks.items()})
    return [blocks[r] for r in range(len(blocks))]


def place_blocks(blocks):
    rows = blocks[0].shape[0]
    count = len(blocks)

    def kernel(mine, *refs):
        for r in range(count):
            first = pl.multiple_of((mine[0] ^ r) * rows, rows)
            refs[count][pl.ds(first, rows)] = refs[r][...]

    return pl.pallas_call(
        kernel,
        out_shape=jax.ShapeDtypeStruct((count * rows,) + blocks[0].shape[1:], blocks[0].dtype),
        in_specs=[pl.BlockSpec(memory_space=pltpu.SMEM)]
        + [pl.BlockSpec(memory_space=pltpu.VMEM)] * count,
        out_specs=pl.BlockSpec(memory_space=pltpu.VMEM),
        name="place",
    )(lax.axis_index("tensor").astype(jnp.int32).reshape(1), *blocks)


def sum_small(values):
    for axis_name in ("tensor", "expert"):
        for b in range(lax.axis_size(axis_name).bit_length() - 1):
            values = values + swap(values, axis_name, 1 << b)
    return values


def sum_expert(values, beside):
    size = lax.axis_size("expert")
    parts = values.astype(LOW).reshape((size, values.shape[0] // size) + values.shape[1:])
    parts = tie(lax.all_to_all(parts, "expert", split_axis=0, concat_axis=0, tiled=True), beside)
    part = jnp.sum(parts.astype(WIDE), axis=0).astype(LOW)
    parts = jnp.broadcast_to(part[None], parts.shape)
    parts = lax.all_to_all(parts, "expert", split_axis=0, concat_axis=0, tiled=True)
    return parts.reshape(values.shape).astype(WIDE)


def pick_rows(near, far, chosen):
    rows = near.shape[0]
    return dot_nn(chosen[:, :rows], near) + dot_nn(chosen[:, rows:], far)


def gelu_pair(values):
    slope = (2.0 / jnp.pi) ** 0.5
    square = values * values
    bend = jnp.tanh(slope * values * (1.0 + 0.044715 * square))
    outer = 0.5 + 0.5 * bend
    steep = slope * (1.0 + 3 * 0.044715 * square)
    return values * outer, outer + 0.5 * values * (1.0 - bend * bend) * steep


def short_rows(rows):
    return rows * 9 // 16 // 16 * 16


def split_low(values, rounded=lambda values: values.astype(LOW).astype(WIDE)):
    pieces = []
    for _ in range(3):
        piece = rounded(values)
        pieces.append(piece.astype(LOW))
        values = values - piece
    return pieces


def round_low(values):
    return lax.reduce_precision(values, 8, 7)


def expert_kernel(blocks, chunk, experts, tokens, joined, meta, near, far, grads, *refs):
    weights, refs = refs[: 2 * blocks], refs[2 * blocks + tokens :]
    (kept_rows, kept_grads, count, hidden_out, pre_out), refs = refs[:5], refs[5:]
    if joined:
        backs, refs = refs[:2], refs[2:]
        mix_outs = None
    else:
        backs, mix_outs, refs = refs[:2], refs[2:4], refs[4:]
    weight_buf, grad_buf, hidden_buf, pre_buf, weight_sem, grad_sem, out_sem = refs
    span = grad_buf.shape[0]
    rows = span // 2
    model_width = near.shape[1]
    mine = meta[0]

    def weight_copy(n):
        return pltpu.make_async_copy(weights[n], weight_buf.at[n], weight_sem.at[n])

    def side_rows(side):
        return pl.ds(pl.multiple_of((mine ^ (2 * chunk + side)) * rows, rows), rows)

    def grad_copy(side):
        return pltpu.make_async_copy(
            grads.at[side_rows(side)], grad_buf.at[pl.ds(side * rows, rows)], grad_sem.at[side]
        )

    for side in (0, 1):
        grad_copy(side).start()
    for n in range(2 * blocks):
        weight_copy(n).start()

    def gates_of(payload):
        extra = payload[rows : rows + experts, :].astype(WIDE)
        here = lax.broadcasted_iota(jnp.int32, extra.shape, 0) == mine
        line = jnp.sum(jnp.where(here, extra, 0.0), axis=0, keepdims=True)
        return line[:, :rows] + line[:, rows : 2 * rows] + line[:, 2 * rows :]

    gate_row = jnp.concatenate([gates_of(near), gates_of(far)], axis=1)
    routed = gate_row != 0.0
    earlier = lax.broadcasted_iota(jnp.int32, (span, span), 0) < lax.broadcasted_iota(
        jnp.int32, (span, span), 1
    )
    routed_wide = routed.astype(WIDE)
    rank = dot_nn(
        jnp.broadcast_to(routed_wide, (8, span)).astype(LOW), earlier.astype(WIDE).astype(LOW)
    )[:1]
    rank = jnp.where(routed, rank, -1.0).astype(jnp.int32)
    total = jnp.sum(routed_wide).astype(jnp.int32)
    count[0] = total

    def run(taken):
        def out_copy(n, buffer, target, lane):
            return pltpu.make_async_copy(
                buffer.at[n, pl.ds(0, taken)], target.at[n, pl.ds(0, taken)], out_sem.at[lane, n]
            )

        chosen_wide = (rank == lax.broadcasted_iota(jnp.int32, (taken, span), 0)).astype(WIDE)
        chosen = chosen_wide.astype(LOW)
        picked = pick_rows(near[:rows], far[:rows], chosen).astype(LOW)
        gate_col = jnp.sum(chosen_wide * gate_row, axis=1, keepdims=True)
        for side in (0, 1):
            grad_copy(side).wait()
        grad_rows = pick_rows(grad_buf[:rows], grad_buf[rows:], chosen)
        gated = (gate_col * grad_rows).astype(LOW)
        kept_rows[:taken] = picked
        kept_grads[:taken] = gated
        expert_out = jnp.zeros((taken, model_width), WIDE)
        row_grad = jnp.zeros((taken, model_width), WIDE)
        for n in range(blocks):
            w_in, w_down = weight_buf.at[2 * n], weight_buf.at[2 * n + 1]
            weight_copy(2 * n).wait()
            weight_copy(2 * n + 1).wait()
            value, slope = gelu_pair(dot_nn(picked, w_in[...]))
            hidden = value.astype(LOW)
            hidden_buf[n, :taken] = hidden
            out_copy(n, hidden_buf, hidden_out, 0).start()
            pre_grad = (dot_nt(gated, w_down[...]) * slope).astype(LOW)
            pre_buf[n, :taken] = pre_grad
            out_copy(n, pre_buf, pre_out, 1).start()
            expert_out = expert_out + dot_nn(hidden, w_down[...]).astype(LOW).astype(WIDE)
            row_grad = row_grad + dot_nt(pre_grad, w_in[...]).astype(LOW).astype(WIDE)
        mixed = dot_tn(chosen, (gate_col * expert_out).astype(LOW)).astype(LOW)
        back = dot_tn(chosen, row_grad.astype(LOW)).astype(LOW)
        grad_col = jnp.sum(grad_rows * expert_out, axis=1, keepdims=True)
        gate_grad = jnp.sum(chosen_wide * grad_col, axis=0, keepdims=True)
        extra = payload_rows(rows, experts) - rows
        for side, back_out in enumerate(backs):
            part = slice(side * rows, (side + 1) * rows)
            back_out[:rows] = back[part]
            pieces = split_low(gate_grad[:, part])
            line = jnp.concatenate([piece.astype(WIDE) for piece in pieces], axis=1)
            here = lax.broadcasted_iota(jnp.int32, (extra, model_width), 0) == mine
            back_out[rows : rows + extra] = jnp.where(here, line, 0.0).astype(LOW)
            if joined:
                back_out[rows + extra :] = mixed[part]
            else:
                mix_outs[side][...] = mixed[part]
        for n in range(blocks):
            out_copy(n, hidden_buf, hidden_out, 0).wait()
            out_copy(n, pre_buf, pre_out, 1).wait()

    few = total <= short_rows(span)

    @pl.when(few)
    def _():
        run(short_rows(span))

    @pl.when(jnp.logical_not(few))
    def _():
        run(span)


def payload_rows(rows, experts):
    return rows + -(-experts // 16) * 16


def expert_chunk(chunk, experts, rows, joined, meta, near, far, grads, weights, tokens):
    payload, model_width = near.shape
    span = 2 * rows
    blocks = len(weights) // 2
    block_width = weights[0].shape[1]
    low = functools.partial(jax.ShapeDtypeStruct, dtype=LOW)
    vmem = pl.BlockSpec(memory_space=pltpu.VMEM)
    smem = pl.BlockSpec(memory_space=pltpu.SMEM)
    sides = [low((payload + rows, model_width))] * 2
    if not joined:
        sides = [low((payload, model_width))] * 2 + [low((rows, model_width))] * 2
    return pl.pallas_call(
        functools.partial(expert_kernel, blocks, chunk, experts, len(tokens), joined),
        out_shape=(
            low((span, model_width)),
            low((span, model_width)),
            jax.ShapeDtypeStruct((1,), jnp.int32),
            low((blocks, span, block_width)),
            low((blocks, span, block_width)),
            *sides,
        ),
        in_specs=[smem, vmem, vmem] + [ANYWHERE] * (1 + len(weights) + len(tokens)),
        out_specs=(vmem, vmem, smem, ANYWHERE, ANYWHERE) + (vmem,) * len(sides),
        scratch_shapes=[
            pltpu.VMEM((2 * blocks,) + weights[0].shape, LOW),
            pltpu.VMEM((span, model_width), LOW),
            pltpu.VMEM((blocks, span, block_width), LOW),
            pltpu.VMEM((blocks, span, block_width), LOW),
            pltpu.SemaphoreType.DMA((2 * blocks,)),
            pltpu.SemaphoreType.DMA((2,)),
            pltpu.SemaphoreType.DMA((2, blocks)),
        ],
        compiler_params=pltpu.CompilerParams(vmem_limit_bytes=VMEM_BYTES),
        cost_estimate=pl.CostEstimate(
            flops=200 * short_rows(span) * model_width * block_width * blocks,
            bytes_accessed=1 << 24,
            transcendentals=0,
        ),
        name="expert_chunk",
    )(meta, near, far, grads, *weights, *tokens)


def weight_grad_kernel(chunks, block, tokens, *refs):
    counts, refs = refs[:chunks], refs[chunks:]
    kept, refs = refs[: 4 * chunks], refs[4 * chunks + tokens :]
    done, refs = refs[0], refs[1:]
    done[0] = counts[0][0]
    if block:
        out_ref, refs = refs[0], refs[1:]
    in_grad, down_grad, row_buf, grad_buf, hidden_buf, pre_buf, sem = refs
    span = row_buf.shape[1]

    def by_count(chunk, action):
        few = counts[chunk][0] <= short_rows(span)

        @pl.when(few)
        def _():
            action(short_rows(span))

        @pl.when(jnp.logical_not(few))
        def _():
            action(span)

    def copies(chunk, taken):
        rows, grads, hidden, pre = kept[4 * chunk : 4 * chunk + 4]
        part = pl.ds(0, taken)
        return [
            pltpu.make_async_copy(source, target, sem.at[chunk, n])
            for n, (source, target) in enumerate(
                (
                    (rows.at[part], row_buf.at[chunk, part]),
                    (grads.at[part], grad_buf.at[chunk, part]),
                    (hidden.at[block, part], hidden_buf.at[chunk, part]),
                    (pre.at[block, part], pre_buf.at[chunk, part]),
                )
            )
        ]

    for chunk in range(chunks):
        by_count(chunk, lambda taken, chunk=chunk: [copy.start() for copy in copies(chunk, taken)])

    def add(chunk, taken):
        for copy in copies(chunk, taken):
            copy.wait()
        in_part = dot_tn(row_buf[chunk, :taken], pre_buf[chunk, :taken])
        down_part = dot_tn(hidden_buf[chunk, :taken], grad_buf[chunk, :taken])
        if chunk == 0:
            in_grad[...] = in_part
            down_grad[...] = down_part
        elif chunk == chunks - 1 and block:
            out_ref[0] = (in_grad[...] + in_part).astype(LOW)
            out_ref[1] = (down_grad[...] + down_part).astype(LOW)
        else:
            in_grad[...] += in_part
            down_grad[...] += down_part

    for chunk in range(chunks):
        by_count(chunk, functools.partial(add, chunk))


def weight_grads(block, counts, kept, tokens):
    chunks = len(kept)
    span, model_width = kept[0][0].shape
    block_width = kept[0][2].shape[2]
    accumulators = [(model_width, block_width), (block_width, model_width)]
    if block:
        out_shape = (jax.ShapeDtypeStruct((2, model_width, block_width), LOW),)
        extra = [pltpu.VMEM(shape, WIDE) for shape in accumulators]
    else:
        out_shape = tuple(jax.ShapeDtypeStruct(shape, WIDE) for shape in accumulators)
        extra = []
    return pl.pallas_call(
        functools.partial(weight_grad_kernel, chunks, block, len(tokens)),
        out_shape=(jax.ShapeDtypeStruct((1,), jnp.int32),) + out_shape,
        out_specs=(pl.BlockSpec(memory_space=pltpu.SMEM),)
        + (pl.BlockSpec(memory_space=pltpu.VMEM),) * len(out_shape),
        in_specs=[pl.BlockSpec(memory_space=pltpu.SMEM)] * chunks
        + [ANYWHERE] * (4 * chunks + len(tokens)),
        scratch_shapes=extra
        + [
            pltpu.VMEM((chunks, span, model_width), LOW),
            pltpu.VMEM((chunks, span, model_width), LOW),
            pltpu.VMEM((chunks, span, block_width), LOW),
            pltpu.VMEM((chunks, span, block_width), LOW),
            pltpu.SemaphoreType.DMA((chunks, 4)),
        ],
        compiler_params=pltpu.CompilerParams(vmem_limit_bytes=VMEM_BYTES),
        cost_estimate=pl.CostEstimate(
            flops=120 * chunks * short_rows(span) * model_width * block_width,
            bytes_accessed=1 << 23,
            transcendentals=0,
        ),
        name="weight_grads",
    )(*counts, *[array for four in kept for array in four], *tokens)


def dense_experts(normed_low, grad_low, gates, choose, routes, gathered):
    rows, model_width = normed_low.shape
    experts = choose.shape[2]
    size = lax.axis_size("expert")
    chunks = size // 2
    meta = lax.axis_index("expert").astype(jnp.int32).reshape(1)
    w_in_blocks, w_down_own, w_down_far, grad_all = gathered
    dense_gates = jnp.sum(gates[:, :, None] * choose, axis=1).T
    gate_rows = jnp.concatenate(split_low(dense_gates, round_low), axis=1)
    payload = jnp.concatenate([normed_low, gate_rows], axis=0)
    payload = jnp.pad(payload, ((0, payload_rows(rows, experts) - payload.shape[0]), (0, 0)))
    run = functools.partial(expert_chunk, rows=rows, experts=experts, meta=meta, grads=grad_all)

    def side_swap(values):
        return swap(values, "expert", 1)

    def plane_swap(chunk, values):
        return swap(values, "expert", 2 * chunk)

    far = [side_swap(payload)]
    near = [payload, plane_swap(1, payload)]
    near[1] = tie(near[1], far[0])
    far.append(side_swap(near[1]))
    near.append(plane_swap(2, tie(payload, near[1])))
    last_down = tie(w_down_far, near[1])
    in_blocks = w_in_blocks
    down_blocks = [w_down_own, swap(w_down_own, "tensor", 1), last_down, swap(last_down, "tensor", 1)]
    weights = [block for pair in zip(in_blocks, down_blocks) for block in pair]

    kept, counts, held, flown, mixes, backs = [], [], [], [], [], []

    def chunk_step(chunk, tokens):
        joined = chunk < 2
        rows_c, grads_c, count, hidden, pre, back_near, back_far, *mixed = run(
            chunk, joined=joined, near=near[chunk], far=far[chunk], weights=weights, tokens=tokens
        )
        kept.append((rows_c, grads_c, hidden, pre))
        counts.append(count)
        mixes.append(mixed)
        backs.append((back_near, side_swap(back_far)))

    def hold(chunk, token):
        back_near, arrived = backs[chunk]
        return (back_near.astype(WIDE) + tie(arrived, token).astype(WIDE)).astype(LOW)

    chunk_step(0, [far[1], near[2]])
    far.append(side_swap(near[2]))
    near.append(plane_swap(3, tie(payload, near[2])))
    chunk_step(1, [counts[0]])
    near[3] = tie(near[3], counts[1])
    far.append(side_swap(near[3]))
    held.append(hold(0, counts[1]))
    chunk_step(2, [counts[1], held[0]])
    held.append(hold(1, counts[2]))
    flown.append(plane_swap(1, held[1]))
    chunk_step(3, [counts[2], held[1]])
    held.append(hold(2, counts[3]))
    flown[0] = tie(flown[0], counts[3])
    flown.append(plane_swap(2, held[2]))
    joint = held[0].astype(WIDE) + flown[0].astype(WIDE)
    grads_of = functools.partial(weight_grads, counts=counts, kept=kept)
    done3, block3 = grads_of(3, tokens=[flown[0], held[2]])
    held.append(hold(3, done3))
    flown.append(plane_swap(3, held[3]))
    core3 = swap(block3, "tensor", 1)
    late = [side_swap(tie(mixes[chunk][1], held[3])) for chunk in (2, 3)]
    done2, block2 = grads_of(2, tokens=[done3, held[3]])
    flown[1] = tie(flown[1], done2)
    flown[2] = tie(flown[2], done2)
    chip_sum = (block2.astype(WIDE) + tie(core3, done2).astype(WIDE)).astype(LOW)
    late = [
        (mixes[chunk][0].astype(WIDE) + tie(arrived, done2).astype(WIDE)).astype(LOW)
        for chunk, arrived in zip((2, 3), late)
    ]
    late = [plane_swap(chunk, values) for chunk, values in zip((2, 3), late)]
    payload = payload.shape[0]
    row_grad = joint[:payload] + flown[1].astype(WIDE) + flown[2].astype(WIDE)
    tail = row_grad[rows : rows + experts]
    gate_grad = tail[:, :rows] + tail[:, rows : 2 * rows] + tail[:, 2 * rows :]
    gate_grad = jnp.sum(gate_grad.T[:, None, :] * choose, axis=-1)

    def early_weights(token):
        return grads_of(1, tokens=[token])

    def send_weights(n, arrived):
        sent = chip_sum[n] if arrived is None else tie(chip_sum[n], arrived)
        return swap(sent, "tensor", 2)

    def finish_mixed(token):
        mixed = joint[payload:]
        for values in late:
            mixed = mixed + tie(values, token).astype(WIDE)
        return mixed

    def finish_weights(block1, token):
        done0, *block0 = grads_of(0, tokens=[token])
        near_sum = tie(swap(block1, "tensor", 1), token)
        return done0, lambda far_sums: tuple(
            (block0[n] + near_sum[n].astype(WIDE) + far_sums[n].astype(WIDE))[None] for n in (0, 1)
        )

    return gate_grad, row_grad[:rows], early_weights, send_weights, finish_mixed, finish_weights


def pick_slots(buffer, flat_experts, slot_index, first_slot, slot_count):
    local_slot = slot_index - first_slot
    inside = ((local_slot >= 0) & (local_slot < slot_count)).astype(WIDE)
    rows = buffer[flat_experts, 0, jnp.clip(local_slot, 0, slot_count - 1)].astype(WIDE)
    return rows * inside[:, None]


def slot_experts(normed_low, grad_low, gates, choose, routes, gathered):
    w_in, w_down = gathered
    own = normed_low.shape[0]
    tensor_size = lax.axis_size("tensor")
    sources = lax.axis_size("expert")
    first_own = lax.axis_index("tensor") * own
    length = own * tensor_size
    experts = choose.shape[2]
    model_width = normed_low.shape[1]
    capacity = 4 * length // experts
    share_rows = capacity // tensor_size
    first_share = lax.axis_index("tensor") * share_rows
    normed_all = lax.all_gather(normed_low, "tensor", axis=0, tiled=True)
    grad_all = lax.all_gather(grad_low, "tensor", axis=0, tiled=True)
    gates_all = lax.all_gather(gates, "tensor", axis=0, tiled=True)
    flat_experts = routes.reshape(-1)
    marks = (flat_experts[:, None] == jnp.arange(experts)[None, :]).astype(jnp.int32)
    slot_index = jnp.sum((jnp.cumsum(marks, axis=0) - 1) * marks, axis=1)
    token_index = jnp.arange(2 * length) // 2

    def send(values):
        empty = jnp.zeros((experts, 1, capacity, model_width), LOW)
        placed = empty.at[flat_experts, 0, slot_index].set(values)
        arrived = lax.all_to_all(placed, "expert", split_axis=0, concat_axis=1, tiled=True)
        return arrived.reshape(sources * capacity, model_width)

    def give_back(values):
        summed = lax.psum_scatter(
            values.reshape(sources, capacity, model_width), "tensor", scatter_dimension=1, tiled=True
        )
        returned = lax.all_to_all(
            summed.reshape(1, sources, share_rows, model_width),
            "expert", split_axis=1, concat_axis=0, tiled=True,
        )
        return pick_slots(returned, flat_experts, slot_index, first_share, share_rows).reshape(
            length, 2, model_width
        )

    expert_rows = send(normed_all[token_index])
    grad_wide = grad_all.astype(WIDE)
    toward = (gates_all[:, :, None] * grad_wide[:, None, :]).astype(LOW)
    grad_rows = send(toward.reshape(2 * length, model_width))
    hidden_pre = dot_nn(expert_rows, w_in[0])
    hidden, gelu_back = jax.vjp(functools.partial(jax.nn.gelu, approximate=True), hidden_pre)
    hidden = hidden.astype(LOW)
    picked = give_back(dot_nn(hidden, w_down[0]).astype(LOW))
    grad_pre = gelu_back(dot_nt(grad_rows, w_down[0]))[0].astype(LOW)
    d_w_down = dot_tn(hidden, grad_rows)[None]
    d_w_in = dot_tn(expert_rows, grad_pre)[None]
    back_rows = give_back(dot_nt(grad_pre, w_in[0]).astype(LOW))
    mixed = jnp.sum(gates_all[:, :, None] * picked, axis=1)
    gate_grad = jnp.sum(picked * grad_wide[:, None, :], axis=-1)
    mixed, gate_grad, row_grad = (
        lax.dynamic_slice_in_dim(values, first_own, own, 0)
        for values in lax.psum((mixed, gate_grad, jnp.sum(back_rows, axis=1)), "tensor")
    )
    token = gate_grad[:1, :1]
    return (
        gate_grad,
        row_grad,
        lambda token: (token, token),
        lambda n, arrived: token,
        lambda token: mixed,
        lambda block1, token: (token, lambda far_sums: (d_w_in, d_w_down)),
    )


def body(
    tokens,
    cotangent,
    gain_attn,
    gain_ffn,
    w_qkv,
    w_out,
    bias_table,
    router,
    w_in,
    w_down,
    routes,
    sequence_ids,
    rel_buckets,
):
    length, model_width = tokens.shape
    rows = min(QUERY_ROWS, length)
    bucket_count, heads = bias_table.shape
    width = w_qkv.shape[2]
    head_size = width // heads
    experts = router.shape[1]
    tensor_size = lax.axis_size("tensor")
    own = length // tensor_size
    mine = lax.axis_index("tensor")

    def own_rows(values):
        return lax.dynamic_slice_in_dim(values, mine * own, own, 0)

    gain_one = gain_attn.astype(WIDE)
    gain_two = gain_ffn.astype(WIDE)
    grad_low = own_rows(cotangent)
    grad_output = grad_low.astype(WIDE)
    own_inputs = own_rows(tokens).astype(WIDE)
    own_routes = own_rows(routes)
    out_blocks = gather_tensor(w_out)

    _, _, normed_one = normalize(tokens.astype(WIDE), gain_one)
    normed_low = normed_one.astype(LOW)
    qkv = jnp.einsum("td,cdh->cth", normed_low, w_qkv, preferred_element_type=WIDE).astype(LOW)
    line_width = length + rows
    place = jnp.arange(line_width)
    distance = jnp.where(place < length, length - rows - place, 2 * length - place)
    buckets = jnp.concatenate(
        [
            rel_buckets[: length - rows + 1][::-1],
            jnp.zeros((rows,), jnp.int32),
            rel_buckets[length - rows + 1 :][::-1],
        ]
    )
    bucket_pick = (
        (buckets[:, None] == jnp.arange(bucket_count)[None, :]) & (distance >= 0)[:, None]
    ).astype(WIDE)
    lines = dot_tn(bias_table.astype(WIDE), bucket_pick.T, PRECISE)
    lines = jnp.where((distance >= 0)[None, :], lines, FLOOR_SCORE)
    ids_col = sequence_ids[:, None]
    ids_row = sequence_ids[None, :]
    mixed_heads, lse = attend(qkv, lines, ids_col, ids_row, heads, head_size, rows)

    whole_width = (
        lax.axis_size("expert") == 8
        and tensor_size == 4
        and 3 * own == model_width
        and w_in.shape[2] == model_width
    )
    if whole_width:
        w_in_far = tie(swap(w_in[0], "tensor", 2), lse)
        w_in_near = swap(w_in[0], "tensor", 1)

    half = [mixed_heads]
    tags = [0]
    span = length
    for bit in reversed(tensor_bits()):
        span //= 2
        keep_at = jnp.where((mine & bit) != 0, span, 0)
        give_at = span - keep_at
        given = [lax.dynamic_slice_in_dim(block, give_at, span, 0) for block in half]
        if whole_width and len(half) == 1:
            given = [tie(given[0], w_in_far)]
        arrived = [swap(block, "tensor", bit) for block in given]
        half = [lax.dynamic_slice_in_dim(block, keep_at, span, 0) for block in half] + arrived
        tags = tags + [tag | bit for tag in tags]
    attention = sum(dot_nn(block, out_blocks[tag]) for tag, block in zip(tags, half))
    middle = own_inputs + attention
    plain_two, scale_two, normed_two = normalize(middle, gain_two)
    router_float = router.astype(WIDE)
    logits = jnp.dot(normed_two, router_float, precision=PRECISE)
    choose = (own_routes[:, :, None] == jnp.arange(experts)[None, None, :]).astype(WIDE)
    chosen = jnp.sum(logits[:, None, :] * choose, axis=-1)
    gates = jax.nn.softmax(chosen, axis=1)

    if whole_width:
        w_down_own = tie(w_down[0], half[1])
        gathered = (
            [w_in[0], w_in_near, w_in_far, swap(w_in_far, "tensor", 1)],
            w_down_own,
            swap(w_down_own, "tensor", 2),
            lax.all_gather(grad_low, "expert", axis=0, tiled=True),
        )
    else:
        gathered = (w_in, w_down)
    run_experts = dense_experts if whole_width else slot_experts
    gate_grad, grad_normed_two, early_weights, send_weights, finish_mixed, finish_weights = run_experts(
        normed_two.astype(LOW), grad_low, gates, choose, routes, gathered
    )

    mean_grad = jnp.sum(gates * gate_grad, axis=1, keepdims=True)
    select_grad = gates * (gate_grad - mean_grad)
    logit_grad = jnp.sum(select_grad[:, :, None] * choose, axis=1)
    grad_normed_two = grad_normed_two + dot_nt(logit_grad, router_float, PRECISE)
    back_two, d_gain_ffn = norm_back(grad_normed_two, plain_two, scale_two, gain_two)
    grad_middle = grad_output + back_two
    own_grad_attn = grad_middle.astype(LOW)
    done1, block1 = early_weights(own_grad_attn)
    grad_blocks = [own_grad_attn]
    for bit in reversed(tensor_bits()):
        arrived = [tie(swap(block, "tensor", bit), done1) for block in grad_blocks]
        grad_blocks = grad_blocks + arrived if len(grad_blocks) == 1 else [
            *(grad_blocks[:1] + arrived[:1] + grad_blocks[1:] + arrived[1:])
        ]
    far_sums = [send_weights(0, None), send_weights(1, grad_blocks[2])]
    grad_attn = place_blocks(grad_blocks)
    sums, grad_one, fold = attend_back(
        qkv, mixed_heads, grad_attn, normed_low, w_qkv, w_out, lse, lines, ids_col, ids_row,
        heads, head_size, rows, [done1, far_sums[0]],
    )
    sums = tie(sums, far_sums[1])
    mixed = finish_mixed(fold)
    d_router = dot_tn(logit_grad, normed_two, PRECISE)
    done0, add_weights = finish_weights(block1, sums)
    sums = sum_expert(sums, done0)
    d_qkv = sums[: 3 * width].reshape(3, width, model_width).transpose(0, 2, 1)
    d_out = sums[3 * width :]
    quarters = [
        lax.dynamic_slice_in_dim(grad_one, (mine ^ r) * own, own, 0) for r in range(tensor_size)
    ]
    held = quarters
    for bit in tensor_bits():
        keep = jnp.concatenate([held[r] for r in range(len(held)) if not r & 1], axis=0)
        give = jnp.concatenate([held[r] for r in range(len(held)) if r & 1], axis=0).astype(LOW)
        arrived = swap(give, "tensor", bit)
        held = keep.astype(WIDE) + arrived.astype(WIDE)
        held = [held[n * own : (n + 1) * own] for n in range(held.shape[0] // own)]
    grad_one = held[0]
    d_w_in, d_w_down = add_weights(far_sums)
    output_rows = place_blocks(gather_tensor((middle + mixed).astype(LOW)))
    plain_one, scale_one, _ = normalize(own_inputs, gain_one)
    back_one, d_gain_attn = norm_back(grad_one, plain_one, scale_one, gain_one)
    d_tokens = place_blocks(gather_tensor((grad_middle + back_one).astype(LOW)))

    d_bias = dot_nn_precise(fold, bucket_pick)
    d_bias = jnp.pad(d_bias, ((0, 0), (0, model_width - bucket_count)))
    here = (jnp.arange(tensor_size) == mine)[:, None, None]
    flat = jnp.concatenate(
        [
            d_gain_attn[None],
            d_gain_ffn[None],
            d_router,
            jnp.where(here, d_bias[None], 0.0).reshape(tensor_size * heads, model_width),
        ],
        axis=0,
    )
    flat = sum_small(flat)
    d_router = flat[2 : 2 + experts].T
    d_bias = lax.dynamic_slice_in_dim(flat, 2 + experts + mine * heads, heads, 0)
    return (
        output_rows,
        d_tokens,
        flat[0],
        flat[1],
        d_qkv,
        d_out,
        d_bias[:, :bucket_count].T,
        d_router,
        d_w_in,
        d_w_down,
    )


def solution(mesh):
    return jax.shard_map(
        body,
        mesh=mesh,
        in_specs=(
            P("expert", None),
            P("expert", None),
            P(),
            P(),
            P(None, None, "tensor"),
            P("tensor", None),
            P(None, "tensor"),
            P(),
            P("expert", None, "tensor"),
            P("expert", "tensor", None),
            P("expert", None),
            P("expert"),
            P(),
        ),
        out_specs=(
            P("expert", None),
            P("expert", None),
            P(),
            P(),
            P(None, None, "tensor"),
            P("tensor", None),
            P(None, "tensor"),
            P(),
            P("expert", None, "tensor"),
            P("expert", "tensor", None),
        ),
        check_vma=False,
    )
```
